256 devices in a mesh: row: 16 (over y, z_hi), col: 16 (over x, z_lo, core).
Axes of the slice: x: 4, y: 4, z: 8 (z_hi: 4, z_lo: 2; z = z_hi * 2 + z_lo), core: 2. Of those that a mesh axis runs over, the one named last changes fastest.
Arguments:
- alignment_left: bfloat16 [1024, 1024], P(('row', 'col')), may hold values from -6 to 6
- alignment_right: bfloat16 [1024, 1024], P(('col', 'row')), may hold values from -6 to 6
- output_weight: bfloat16 [1024, 128], replicated, may hold values from -0.1875 to 0.1875
- bias: float32 [128], replicated, may hold values from -3 to 3
- cotangent: bfloat16 [1024, 1024, 128], P('row', 'col'), may hold values from -6 to 6
Outputs:
- pair: bfloat16 [1024, 1024, 128], P('row', 'col')
- grad_left: bfloat16 [1024, 1024], P(('row', 'col'))
- grad_right: bfloat16 [1024, 1024], P(('col', 'row'))
- grad_w: float32 [1024, 128], P(('row', 'col'))
The draws below stay inside these ranges and needn't reach their ends.
All inputs are finite; a program needn't handle non-finite values.
Results may differ from the reference program's by a relative error of at most 0.0049.
Values may be sent and summed in bfloat16 or wider, within the bound.
A program may use at most 128 MiB of HBM per device.

```python
import jax
import jax.numpy as jnp
from jax import lax

LEFT_CHANNELS = 32
RIGHT_CHANNELS = 32
CZ = 128
SEQUENCE_COUNT = 32
RESIDUE_COUNT = 1024


def shard_levels(stream_key, dims, cuts, least, top_value):
    factor_of, own = 1.0, jax.random.fold_in(stream_key, 6)
    for axis_at, blocks in cuts:
        steps = jnp.exp(jax.random.uniform(jax.random.fold_in(own, axis_at), (blocks,), jnp.float32, least / len(cuts), top_value / len(cuts)))
        factor_of = factor_of * jnp.repeat(steps, dims[axis_at] // blocks).reshape([-1 if axis == axis_at else 1 for axis in range(len(dims))])
    return factor_of


def noise(own_key, dims, width, limit, pieces=(), dtype=jnp.bfloat16):
    drawn = jax.random.normal(own_key, dims, jnp.float32) * width
    if len(pieces) > 0:
        drawn = shard_levels(own_key, dims, pieces, -0.22, 0.18) * drawn
    return jnp.clip(drawn, min=-limit, max=limit).astype(dtype)


def setup_inputs(seed: int = 0) -> dict:
    key_list = jax.random.split(jax.random.key(seed), 6)
    alignment_left = noise(key_list[0], (RESIDUE_COUNT, SEQUENCE_COUNT * LEFT_CHANNELS), 1.0, 6.0, ((0, 256),))
    alignment_right = noise(key_list[1], (RESIDUE_COUNT, SEQUENCE_COUNT * RIGHT_CHANNELS), 1.0, 6.0, ((0, 256),))
    output_weight = noise(key_list[2], (LEFT_CHANNELS * RIGHT_CHANNELS, CZ), (LEFT_CHANNELS * RIGHT_CHANNELS) ** -0.5, 0.1875)
    bias = noise(key_list[3], (CZ,), 0.5, 3.0, (), jnp.float32)
    cotangent = noise(key_list[4], (RESIDUE_COUNT, RESIDUE_COUNT, CZ), 1.0, 6.0, ((0, 16), (1, 16)))
    return dict(alignment_left=alignment_left, alignment_right=alignment_right, output_weight=output_weight, bias=bias, cotangent=cotangent)


def reference(alignment_left, alignment_right, output_weight, bias, cotangent):
    left_input = alignment_left.reshape(RESIDUE_COUNT, SEQUENCE_COUNT, LEFT_CHANNELS).astype(jnp.float32)
    right_input = alignment_right.reshape(RESIDUE_COUNT, SEQUENCE_COUNT, RIGHT_CHANNELS).astype(jnp.float32)
    block = min(32, RESIDUE_COUNT)
    count = RESIDUE_COUNT // block
    left_blocks = left_input.reshape(count, block, SEQUENCE_COUNT, LEFT_CHANNELS)
    cot_blocks = cotangent.reshape(count, block, RESIDUE_COUNT, CZ)
    w_wide = output_weight.astype(jnp.float32)

    def step(carry, item):
        grad_w, grad_r = carry
        a_blk, g_blk = item
        outer = jnp.einsum("isc,jsd->ijcd", a_blk, right_input) / SEQUENCE_COUNT
        outer = outer.reshape(block * RESIDUE_COUNT, LEFT_CHANNELS * RIGHT_CHANNELS).astype(jnp.bfloat16)
        pair_blk = jnp.dot(outer, output_weight, preferred_element_type=jnp.float32) + bias
        g_flat = g_blk.reshape(block * RESIDUE_COUNT, CZ)
        g_outer = jnp.dot(g_flat.astype(jnp.float32), w_wide.T).astype(jnp.bfloat16)
        grad_w = grad_w + jnp.dot(outer.astype(jnp.float32).T, g_flat.astype(jnp.float32))
        g_four = g_outer.astype(jnp.float32).reshape(block, RESIDUE_COUNT, LEFT_CHANNELS, RIGHT_CHANNELS)
        ga_blk = jnp.einsum("ijcd,jsd->isc", g_four, right_input)
        grad_r = grad_r + jnp.einsum("ijcd,isc->jsd", g_four, a_blk)
        return (grad_w, grad_r), (pair_blk.astype(jnp.bfloat16).reshape(block, RESIDUE_COUNT, CZ), ga_blk)

    start = (jnp.zeros((LEFT_CHANNELS * RIGHT_CHANNELS, CZ), jnp.float32), jnp.zeros((RESIDUE_COUNT, SEQUENCE_COUNT, RIGHT_CHANNELS), jnp.float32))
    (grad_w, grad_r), (pair, grad_l) = lax.scan(step, start, (left_blocks, cot_blocks))
    pair = pair.reshape(RESIDUE_COUNT, RESIDUE_COUNT, CZ)
    grad_left = (grad_l.reshape(RESIDUE_COUNT, SEQUENCE_COUNT * LEFT_CHANNELS) / SEQUENCE_COUNT).astype(jnp.bfloat16)
    grad_right = (grad_r.reshape(RESIDUE_COUNT, SEQUENCE_COUNT * RIGHT_CHANNELS) / SEQUENCE_COUNT).astype(jnp.bfloat16)
    return pair, grad_left, grad_right, grad_w
```

```python
import functools

import jax
import jax.numpy as jnp
from jax import lax
from jax.experimental import pallas as pl
from jax.experimental.pallas import tpu as pltpu
from jax.sharding import PartitionSpec as P

MESH = pl.DeviceIdType.MESH
BF, F32 = jnp.bfloat16, jnp.float32
S, C, D, Z = 32, 32, 32, 128
N = 16
L = 4
R = N * L
SCALE = 1.0 / S


def dot(a, b):
    return jnp.dot(a, b, preferred_element_type=F32)


def iota(shape, dim):
    return lax.broadcasted_iota(jnp.int32, shape, dim)


def kernel(
    a_ref, b_ref, w_ref, bias_ref, x_hbm, pair_hbm, gl_ref, gr_ref, gw_ref,
    x, xt, wp, wpt, w32, mask, g, o, arep, arept, bp, bpt, b32, bs32,
    gw, gwt, gr, gs32, pairv,
    a_all, b_all, w1_out, w1_in, w2_out, w2_in, l_out, l_in, r_out, r_in,
    x_sem, p_sem, send, recv,
):
    row, col = lax.axis_index("row"), lax.axis_index("col")

    def on_col(k):
        return (row, k)

    def on_row(k):
        return (k, col)

    def push(src, dst, which, device):
        pltpu.make_async_remote_copy(
            src_ref=src, dst_ref=dst, send_sem=send.at[which], recv_sem=recv.at[which],
            device_id=device, device_id_type=MESH,
        ).start()

    def others(me, body):
        def step(t, carry):
            body(lax.rem(me + t, N))
            return carry

        lax.fori_loop(1, N, step, 0)

    def wait_all(ref, sem):
        blocks = ref.at[pl.ds(0, N - 1)]
        pltpu.make_async_copy(blocks, blocks, sem).wait()

    A, B, W1, W2, GL, GR = range(6)

    barrier = pltpu.get_barrier_semaphore()

    def greet(k, to):
        pl.semaphore_signal(barrier, inc=1, device_id=to(k), device_id_type=MESH)

    others(col, lambda k: greet(k, on_col))
    others(row, lambda k: greet(k, on_row))

    def x_load(q):
        part = pl.ds(q * 16, 16)
        return pltpu.make_async_copy(x_hbm.at[part], x.at[part], x_sem.at[q])

    for q in range(4):
        x_load(q).start()
    a_all[col] = a_ref[...]
    b_all[row] = b_ref[...]

    pl.semaphore_wait(barrier, 2 * (N - 1))
    others(row, lambda k: push(b_ref, b_all.at[row], B, on_row(k)))
    others(col, lambda k: push(a_ref, a_all.at[col], A, on_col(k)))

    w32[...] = w_ref[...].astype(F32)
    for d in range(D):
        wp[pl.ds(d * C, C), :] = w32[pl.ds(d, C, stride=D), :].astype(BF)
    for q in range(8):
        wpt[:, pl.ds(q * 128, 128)] = wp[pl.ds(q * 128, 128), :].T
    mask[...] = (iota((256, 256), 0) // 32 == iota((256, 256), 1) // 32).astype(F32).astype(BF)

    for q in range(4):
        x_load(q).wait()

    def outer_grad(q, carry):
        rows = x[pl.ds(q * 8, 8)].reshape(8 * R, Z)
        for dh in range(4):
            part = dot(rows, wpt[:, pl.ds(dh * 256, 256)]).astype(BF)
            g[pl.ds(q * 8, 8), pl.ds(dh * R, R), :] = part.reshape(8, R, 256)
        return carry

    lax.fori_loop(0, 8, outer_grad, 0)

    def x_transpose(q, carry):
        for h in range(4):
            rows = x[pl.ds(q * 16 + h * 4, 4)].reshape(256, Z)
            xt[q, :, pl.ds(h * 256, 256)] = rows.T
        return carry

    lax.fori_loop(0, 4, x_transpose, 0)

    wait_all(b_all, recv.at[B])
    wait_all(a_all, recv.at[A])
    bs32[...] = b_all[...].astype(F32)
    for q in range(N):
        for dh in range(4):
            b32[pl.ds(dh * R + q * L, L), :] = bs32[q, pl.ds(dh * L, L), :]
    bp[...] = b32[...].astype(BF)
    bpt[...] = b32[...].T.astype(BF)

    spread = jnp.where(
        (iota((128, 1024), 0) // 32 == iota((128, 1024), 1) // 256)
        & (iota((128, 1024), 0) % 32 == iota((128, 1024), 1) % 32), SCALE, 0.0).astype(BF)
    arep[...] = dot(a_all[...].reshape(N * S, 128), spread).astype(BF).reshape(N, S, 1024)
    spread_t = jnp.where(iota((32, 256), 0) == iota((32, 256), 1) % 32, SCALE, 0.0).astype(BF)

    def transposed(q, carry):
        arept[q] = dot(a_all[q].astype(F32).T.astype(BF), spread_t).astype(BF)
        return carry

    lax.fori_loop(0, N, transposed, 0)

    def diagonal(block):
        return jnp.concatenate([block] * 8, axis=0) * mask[...]

    def outer(q, carry):
        for i in range(L):
            o[q * L + i] = dot(bp[...], diagonal(arep[q, :, pl.ds(i * 256, 256)])).astype(BF)
        return carry

    lax.fori_loop(0, N, outer, 0)

    for q in range(4):
        for dh in range(4):
            rows = o[pl.ds(q * 16, 16), pl.ds(dh * R, R), :].reshape(16 * R, 256)
            part = dot(xt[q], rows)
            if q == 0:
                gw[:, pl.ds(dh * 256, 256)] = part
            else:
                gw[:, pl.ds(dh * 256, 256)] += part
    for q in range(8):
        gwt[pl.ds(q * 128, 128), :] = gw[:, pl.ds(q * 128, 128)].T
    for k in range(N):
        for dl in range(4):
            first = (4 * (k % 8) + dl) * C + k // 8
            w1_out[k, pl.ds(dl * 16, 16), :] = gwt[pl.ds(first, 16, stride=2), :].astype(BF)
    w1_in[col] = w1_out[col]
    others(col, lambda k: push(w1_out.at[k], w1_in.at[col], W1, on_col(k)))

    gr[...] = jnp.zeros_like(gr)

    def right_grad(q, carry):
        total = gr[...]
        for i in range(L):
            total += dot(g[q * L + i], diagonal(arept[q, pl.ds(i * 32, 32), :]))
        gr[...] = total
        return carry

    lax.fori_loop(0, N, right_grad, 0)
    for q in range(N):
        for dh in range(4):
            gs32[q, pl.ds(dh * L, L), :] = gr[pl.ds(dh * R + q * L, L), :]
    r_out[...] = gs32[...].astype(BF)
    r_in[row] = r_out[row]
    others(row, lambda k: push(r_out.at[k], r_in.at[row], GR, on_row(k)))

    lane4 = iota((32, 256), 1) % 128 // 32
    lane = iota((32, 128), 1) // 32

    def left_group(q):
        result = jnp.zeros((32, 128), F32)
        for pair in range(2):
            i0 = q * L + pair * 2
            both = jnp.zeros((32, 256), F32)
            for h in range(2):
                half = pl.ds(h * 128, 128)
                rhs = jnp.concatenate([g[i0, :, half], g[i0 + 1, :, half]], axis=1)
                part = dot(bpt[half, :], rhs)
                kept = part[96:128]
                for dl in range(3):
                    kept = jnp.where(lane4 == dl, part[dl * 32 : dl * 32 + 32], kept)
                both += kept
            for i in range(2):
                one = both[:, i * 128 : i * 128 + 128]
                one = one + pltpu.roll(one, 64, 1)
                one = one + pltpu.roll(one, 32, 1)
                result = jnp.where(lane == pair * 2 + i, one, result)
        l_out[q] = result.astype(BF)

    def left_step(t, carry):
        q = lax.rem(col + t, N)
        left_group(q)
        push(l_out.at[q], l_in.at[col], GL, on_col(q))
        return carry

    lax.fori_loop(1, N, left_step, 0)
    left_group(col)
    l_in[col] = l_out[col]

    wait_all(w1_in, recv.at[W1])
    total = w1_in[0].astype(F32)
    for k in range(1, N):
        total += w1_in[k].astype(F32)
    gwt[pl.ds(0, 64), :] = total
    for k in range(N):
        w2_out[k] = jnp.concatenate([gwt[pl.ds(k, 4, stride=16), :]] * 2, axis=0)
    w2_in[row] = w2_out[row]
    others(row, lambda k: push(w2_out.at[k], w2_in.at[row], W2, on_row(k)))

    def pair_store(q):
        part = pl.ds(q * 8, 8)
        return pltpu.make_async_copy(pairv.at[part], pair_hbm.at[part], p_sem.at[q])

    def pair_block(q, carry):
        total = jnp.broadcast_to(bias_ref[...], (8 * R, Z))
        for dh in range(4):
            rows = o[pl.ds(q * 8, 8), pl.ds(dh * R, R), :].reshape(8 * R, 256)
            total += dot(rows, wp[pl.ds(dh * 256, 256), :])
        pairv[pl.ds(q * 8, 8)] = total.astype(BF).reshape(8, R, Z)
        pair_store(q).start()
        return carry

    lax.fori_loop(0, 8, pair_block, 0)

    wait_all(r_in, recv.at[GR])
    total = r_in[0].astype(F32)
    for k in range(1, N):
        total += r_in[k].astype(F32)
    gr_ref[...] = total.astype(BF)
    wait_all(l_in, recv.at[GL])
    total = l_in[0].astype(F32)
    for k in range(1, N):
        total += l_in[k].astype(F32)
    gl_ref[...] = (total * SCALE).astype(BF)
    wait_all(w2_in, recv.at[W2])
    total = w2_in[0]
    for k in range(1, N):
        total += w2_in[k]
    gw_ref[...] = total[0:4]

    for ref, which in ((a_all, A), (b_all, B), (w1_in, W1), (w2_in, W2), (l_in, GL), (r_in, GR)):
        wait_all(ref, send.at[which])

    def drain(q, carry):
        pair_store(q).wait()
        return carry

    lax.fori_loop(0, 8, drain, 0)


def shards(a, b, w, bias, x):
    a = a.reshape(L, S, C).transpose(1, 0, 2).reshape(S, L * C)
    b = b.reshape(L, S, 4, 8).transpose(2, 0, 3, 1).reshape(4 * L, 8 * S)
    vmem = pl.BlockSpec(memory_space=pltpu.VMEM)
    hbm = pl.BlockSpec(memory_space=pl.ANY)
    v = pltpu.VMEM
    pair, gl, gr, gw = pl.pallas_call(
        kernel,
        out_shape=(
            jax.ShapeDtypeStruct((R, R, Z), BF),
            jax.ShapeDtypeStruct((S, L * C), BF),
            jax.ShapeDtypeStruct((4 * L, 8 * S), BF),
            jax.ShapeDtypeStruct((4, Z), F32),
        ),
        in_specs=[vmem, vmem, vmem, vmem, hbm],
        out_specs=(hbm, vmem, vmem, vmem),
        scratch_shapes=[
            v((R, R, Z), BF), v((4, Z, 1024), BF), v((1024, Z), BF), v((Z, 1024), BF), v((1024, Z), F32),
            v((256, 256), BF), v((R, 256, 256), BF), v((R, 256, 256), BF),
            v((N, S, 1024), BF), v((N, 128, 256), BF),
            v((256, 256), BF), v((256, 256), BF), v((256, 256), F32), v((N, 16, 256), F32),
            v((Z, 1024), F32), v((1024, Z), F32), v((256, 256), F32), v((N, 16, 256), F32),
            v((R, R, Z), BF),
            v((N, S, 128), BF), v((N, 16, 256), BF),
            v((N, 64, Z), BF), v((N, 64, Z), BF), v((N, 8, Z), F32), v((N, 8, Z), F32),
            v((N, S, 128), BF), v((N, S, 128), BF), v((N, 16, 256), BF), v((N, 16, 256), BF),
            pltpu.SemaphoreType.DMA((4,)), pltpu.SemaphoreType.DMA((8,)),
            pltpu.SemaphoreType.DMA((6,)), pltpu.SemaphoreType.DMA((6,)),
        ],
        compiler_params=pltpu.CompilerParams(
            collective_id=0, has_side_effects=True, vmem_limit_bytes=48 * 2**20
        ),
        cost_estimate=pl.CostEstimate(
            flops=8_000_000_000, bytes_accessed=3_000_000, transcendentals=0
        ),
    )(a, b, w, bias.reshape(1, Z), x)
    gl = gl.reshape(S, L, C).transpose(1, 0, 2).reshape(L, S * C)
    gr = gr.reshape(4, L, 8, S).transpose(1, 3, 0, 2).reshape(L, S * D)
    return pair, gl, gr, gw


def solution(mesh):
    in_specs = (P(("row", "col"), None), P(("col", "row"), None), P(), P(), P("row", "col", None))
    out_specs = (
        P("row", "col", None),
        P(("row", "col"), None),
        P(("col", "row"), None),
        P(("row", "col"), None),
    )
    return jax.shard_map(shards, mesh=mesh, in_specs=in_specs, out_specs=out_specs, check_vma=False)
```

```python
import functools

import jax
import jax.numpy as jnp
from jax import lax
from jax.experimental import pallas as pl
from jax.experimental.pallas import tpu as pltpu
from jax.sharding import PartitionSpec as P

MESH = pl.DeviceIdType.MESH
BF, F32 = jnp.bfloat16, jnp.float32
S, C, D, Z = 32, 32, 32, 128
N = 16
L = 4
R = N * L
SCALE = 1.0 / S


def dot(a, b):
    return jnp.dot(a, b, preferred_element_type=F32)


def iota(shape, dim):
    return lax.broadcasted_iota(jnp.int32, shape, dim)


def kernel(
    a_ref, b_ref, w_ref, bias_ref, x_hbm, pair_hbm, gl_ref, gr_ref, gw_ref,
    x, xt, wp, wpt, w32, mask, g, o, arep, arept, bp, bpt, b32, bs32,
    gw, gwt, gr, gs32, pairv,
    a_all, b_all, w1_out, w1_in, w2_out, w2_in, l_out, l_in, r_out, r_in,
    x_sem, p_sem, send, recv,
):
    row, col = lax.axis_index("row"), lax.axis_index("col")

    def on_col(k):
        return (row, k)

    def on_row(k):
        return (k, col)

    def push(src, dst, which, device):
        pltpu.make_async_remote_copy(
            src_ref=src, dst_ref=dst, send_sem=send.at[which], recv_sem=recv.at[which],
            device_id=device, device_id_type=MESH,
        ).start()

    def others(me, body):
        def step(t, carry):
            body(lax.rem(me + t, N))
            return carry

        lax.fori_loop(1, N, step, 0)

    def wait_all(ref, sem):
        blocks = ref.at[pl.ds(0, N - 1)]
        pltpu.make_async_copy(blocks, blocks, sem).wait()

    A, B, W1, W2, GL, GR = range(6)

    barrier = pltpu.get_barrier_semaphore()

    def greet(k, to):
        pl.semaphore_signal(barrier, inc=1, device_id=to(k), device_id_type=MESH)

    others(col, lambda k: greet(k, on_col))
    others(row, lambda k: greet(k, on_row))

    def x_load(q):
        part = pl.ds(q * 16, 16)
        return pltpu.make_async_copy(x_hbm.at[part], x.at[part], x_sem.at[q])

    for q in range(4):
        x_load(q).start()
    a_all[col] = a_ref[...]
    b_all[row] = b_ref[...]

    pl.semaphore_wait(barrier, 2 * (N - 1))
    others(row, lambda k: push(b_ref, b_all.at[row], B, on_row(k)))
    others(col, lambda k: push(a_ref, a_all.at[col], A, on_col(k)))

    w32[...] = w_ref[...].astype(F32)
    for d in range(D):
        wp[pl.ds(d * C, C), :] = w32[pl.ds(d, C, stride=D), :].astype(BF)
    for q in range(8):
        wpt[:, pl.ds(q * 128, 128)] = wp[pl.ds(q * 128, 128), :].T
    mask[...] = (iota((256, 256), 0) // 32 == iota((256, 256), 1) // 32).astype(F32).astype(BF)

    for q in range(4):
        x_load(q).wait()

    def outer_grad(q, carry):
        rows = x[pl.ds(q * 16, 16)].reshape(16 * R, Z)
        part = dot(rows, wpt[...]).astype(BF)
        for dh in range(4):
            g[pl.ds(q * 16, 16), pl.ds(dh * R, R), :] = part[:, dh * 256 : dh * 256 + 256].reshape(16, R, 256)
        return carry

    lax.fori_loop(0, 4, outer_grad, 0)

    def x_transpose(q, carry):
        for h in range(4):
            rows = x[pl.ds(q * 16 + h * 4, 4)].reshape(256, Z)
            xt[q, :, pl.ds(h * 256, 256)] = rows.T
        return carry

    lax.fori_loop(0, 4, x_transpose, 0)

    wait_all(b_all, recv.at[B])
    wait_all(a_all, recv.at[A])
    bs32[...] = b_all[...].astype(F32)
    for q in range(N):
        for dh in range(4):
            b32[pl.ds(dh * R + q * L, L), :] = bs32[q, pl.ds(dh * L, L), :]
    bp[...] = b32[...].astype(BF)
    bpt[...] = b32[...].T.astype(BF)

    spread = jnp.where(
        (iota((128, 1024), 0) // 32 == iota((128, 1024), 1) // 256)
        & (iota((128, 1024), 0) % 32 == iota((128, 1024), 1) % 32), SCALE, 0.0).astype(BF)
    arep[...] = dot(a_all[...].reshape(N * S, 128), spread).astype(BF).reshape(N, S, 1024)
    for q in range(4):
        turned = a_all[pl.ds(q * 4, 4)].reshape(128, 128).T
        arept[q] = dot(turned, spread).astype(BF)

    def diagonal(block):
        return jnp.concatenate([block] * 8, axis=0) * mask[...]

    def outer(q, carry):
        for t in range(4):
            for i in range(L):
                rhs = diagonal(arep[q * 4 + t, :, pl.ds(i * 256, 256)])
                o[q * 16 + t * 4 + i] = dot(bp[...], rhs).astype(BF)
        return carry

    lax.fori_loop(0, 4, outer, 0)

    for q in range(4):
        for dh in range(4):
            rows = o[pl.ds(q * 16, 16), pl.ds(dh * R, R), :].reshape(16 * R, 256)
            part = dot(xt[q], rows)
            if q == 0:
                gw[:, pl.ds(dh * 256, 256)] = part
            else:
                gw[:, pl.ds(dh * 256, 256)] += part
    for q in range(8):
        gwt[pl.ds(q * 128, 128), :] = gw[:, pl.ds(q * 128, 128)].T
    for k in range(N):
        for dl in range(4):
            first = (4 * (k % 8) + dl) * C + k // 8
            w1_out[k, pl.ds(dl * 16, 16), :] = gwt[pl.ds(first, 16, stride=2), :].astype(BF)
    w1_in[col] = w1_out[col]
    others(col, lambda k: push(w1_out.at[k], w1_in.at[col], W1, on_col(k)))

    gr[...] = jnp.zeros_like(gr)

    def right_grad(q, carry):
        lhs = jnp.concatenate([g[q * 16 + i] for i in range(16)], axis=1)
        rhs = jnp.concatenate(
            [diagonal(arept[q, pl.ds(i % 4 * 32, 32), pl.ds(i // 4 * 256, 256)]) for i in range(16)], axis=0
        )
        gr[...] += dot(lhs, rhs)
        return carry

    lax.fori_loop(0, 4, right_grad, 0)
    for q in range(N):
        for dh in range(4):
            gs32[q, pl.ds(dh * L, L), :] = gr[pl.ds(dh * R + q * L, L), :]
    r_out[...] = gs32[...].astype(BF)
    r_in[row] = r_out[row]
    others(row, lambda k: push(r_out.at[k], r_in.at[row], GR, on_row(k)))

    lane4 = iota((32, 256), 1) % 128 // 32
    lane = iota((32, 128), 1) // 32

    def left_group(q):
        result = jnp.zeros((32, 128), F32)
        for pair in range(2):
            i0 = q * L + pair * 2
            both = jnp.zeros((32, 256), F32)
            for h in range(2):
                half = pl.ds(h * 128, 128)
                rhs = jnp.concatenate([g[i0, :, half], g[i0 + 1, :, half]], axis=1)
                part = dot(bpt[half, :], rhs)
                kept = part[96:128]
                for dl in range(3):
                    kept = jnp.where(lane4 == dl, part[dl * 32 : dl * 32 + 32], kept)
                both += kept
            for i in range(2):
                one = both[:, i * 128 : i * 128 + 128]
                one = one + pltpu.roll(one, 64, 1)
                one = one + pltpu.roll(one, 32, 1)
                result = jnp.where(lane == pair * 2 + i, one, result)
        l_out[q] = result.astype(BF)

    def left_step(u, carry):
        for v in range(4):
            left_group(lax.rem(col + 4 * u + v + 1, N))
        for v in range(4):
            t = 4 * u + v + 1
            q = lax.rem(col + t, N)

            @pl.when(t < N)
            def _():
                push(l_out.at[q], l_in.at[col], GL, on_col(q))

        return carry

    lax.fori_loop(0, 4, left_step, 0)
    l_in[col] = l_out[col]

    wait_all(w1_in, recv.at[W1])
    total = w1_in[0].astype(F32)
    for k in range(1, N):
        total += w1_in[k].astype(F32)
    gwt[pl.ds(0, 64), :] = total
    for k in range(N):
        w2_out[k] = jnp.concatenate([gwt[pl.ds(k, 4, stride=16), :]] * 2, axis=0)
    w2_in[row] = w2_out[row]
    others(row, lambda k: push(w2_out.at[k], w2_in.at[row], W2, on_row(k)))

    def pair_store(q):
        part = pl.ds(q * 8, 8)
        return pltpu.make_async_copy(pairv.at[part], pair_hbm.at[part], p_sem.at[q])

    for q in range(16):
        lhs = jnp.concatenate(
            [o[pl.ds(q * 4, 4), pl.ds(dh * R, R), :].reshape(4 * R, 256) for dh in range(4)], axis=1
        )
        total = dot(lhs, wp[...]) + bias_ref[...]
        pairv[pl.ds(q * 4, 4)] = total.astype(BF).reshape(4, R, Z)
        if q % 2:
            pair_store(q // 2).start()

    wait_all(r_in, recv.at[GR])
    total = r_in[0].astype(F32)
    for k in range(1, N):
        total += r_in[k].astype(F32)
    gr_ref[...] = total.astype(BF)
    wait_all(l_in, recv.at[GL])
    total = l_in[0].astype(F32)
    for k in range(1, N):
        total += l_in[k].astype(F32)
    gl_ref[...] = (total * SCALE).astype(BF)
    wait_all(w2_in, recv.at[W2])
    total = w2_in[0]
    for k in range(1, N):
        total += w2_in[k]
    gw_ref[...] = total[0:4]

    for ref, which in ((a_all, A), (b_all, B), (w1_in, W1), (w2_in, W2), (l_in, GL), (r_in, GR)):
        wait_all(ref, send.at[which])

    def drain(q, carry):
        pair_store(q).wait()
        return carry

    lax.fori_loop(0, 8, drain, 0)


def shards(a, b, w, bias, x):
    a = a.reshape(L, S, C).transpose(1, 0, 2).reshape(S, L * C)
    b = b.reshape(L, S, 4, 8).transpose(2, 0, 3, 1).reshape(4 * L, 8 * S)
    vmem = pl.BlockSpec(memory_space=pltpu.VMEM)
    hbm = pl.BlockSpec(memory_space=pl.ANY)
    v = pltpu.VMEM
    pair, gl, gr, gw = pl.pallas_call(
        kernel,
        out_shape=(
            jax.ShapeDtypeStruct((R, R, Z), BF),
            jax.ShapeDtypeStruct((S, L * C), BF),
            jax.ShapeDtypeStruct((4 * L, 8 * S), BF),
            jax.ShapeDtypeStruct((4, Z), F32),
        ),
        in_specs=[vmem, vmem, vmem, vmem, hbm],
        out_specs=(hbm, vmem, vmem, vmem),
        scratch_shapes=[
            v((R, R, Z), BF), v((4, Z, 1024), BF), v((1024, Z), BF), v((Z, 1024), BF), v((1024, Z), F32),
            v((256, 256), BF), v((R, 256, 256), BF), v((R, 256, 256), BF),
            v((N, S, 1024), BF), v((4, 128, 1024), BF),
            v((256, 256), BF), v((256, 256), BF), v((256, 256), F32), v((N, 16, 256), F32),
            v((Z, 1024), F32), v((1024, Z), F32), v((256, 256), F32), v((N, 16, 256), F32),
            v((R, R, Z), BF),
            v((N, S, 128), BF), v((N, 16, 256), BF),
            v((N, 64, Z), BF), v((N, 64, Z), BF), v((N, 8, Z), F32), v((N, 8, Z), F32),
            v((N, S, 128), BF), v((N, S, 128), BF), v((N, 16, 256), BF), v((N, 16, 256), BF),
            pltpu.SemaphoreType.DMA((4,)), pltpu.SemaphoreType.DMA((8,)),
            pltpu.SemaphoreType.DMA((6,)), pltpu.SemaphoreType.DMA((6,)),
        ],
        compiler_params=pltpu.CompilerParams(
            collective_id=0, has_side_effects=True, vmem_limit_bytes=48 * 2**20
        ),
        cost_estimate=pl.CostEstimate(
            flops=8_000_000_000, bytes_accessed=3_000_000, transcendentals=0
        ),
    )(a, b, w, bias.reshape(1, Z), x)
    gl = gl.reshape(S, L, C).transpose(1, 0, 2).reshape(L, S * C)
    gr = gr.reshape(4, L, 8, S).transpose(1, 3, 0, 2).reshape(L, S * D)
    return pair, gl, gr, gw


def solution(mesh):
    in_specs = (P(("row", "col"), None), P(("col", "row"), None), P(), P(), P("row", "col", None))
    out_specs = (
        P("row", "col", None),
        P(("row", "col"), None),
        P(("col", "row"), None),
        P(("row", "col"), None),
    )
    return jax.shard_map(shards, mesh=mesh, in_specs=in_specs, out_specs=out_specs, check_vma=False)
```

```python
import jax
import jax.numpy as jnp
from jax import lax
from jax.experimental import pallas as pl
from jax.experimental.pallas import tpu as pltpu
from jax.sharding import PartitionSpec as P

MESH = pl.DeviceIdType.MESH
BF, F32 = jnp.bfloat16, jnp.float32
S, C, D, Z = 32, 32, 32, 128
N = 16
L = 4
R = N * L
SCALE = 1.0 / S


def dot(a, b):
    return jnp.dot(a, b, preferred_element_type=F32)


def iota(shape, dim):
    return lax.broadcasted_iota(jnp.int32, shape, dim)


def one_hot(condition):
    return jnp.where(condition, 1.0, 0.0).astype(BF)


def kernel(
    a_hbm, b_hbm, w_hbm, bias_hbm, x_hbm, pair, gl_ref, gr_ref, gw_ref,
    a_own, b_own, w_own, bias, x, xt, wp, wpt, w32, mask, g, o, arep, arept, bp, bpt, b32, bs32,
    gwt, gr, gs32, rows32, fold, gather_s,
    a_all, b_all, w1_out, w1_in, w2_out, w2_in, l_out, l_in, r_out, r_in,
    own_sem, x_sem, send, recv,
):
    row, col = lax.axis_index("row"), lax.axis_index("col")

    def on_col(k):
        return (row, k)

    def on_row(k):
        return (k, col)

    def push(src, dst, which, device):
        pltpu.make_async_remote_copy(
            src_ref=src, dst_ref=dst, send_sem=send.at[which], recv_sem=recv.at[which],
            device_id=device, device_id_type=MESH,
        ).start()

    def others(me, body):
        def step(t, carry):
            body(lax.rem(me + t, N))
            return carry

        lax.fori_loop(1, N, step, 0)

    def wait_all(ref, sem):
        blocks = ref.at[pl.ds(0, N - 1)]
        pltpu.make_async_copy(blocks, blocks, sem).wait()

    A, B, W1, W2, GL, GR = range(6)

    loads = [
        pltpu.make_async_copy(src, dst, own_sem.at[n])
        for n, (src, dst) in enumerate(((a_hbm, a_own), (b_hbm, b_own), (w_hbm, w_own), (bias_hbm, bias)))
    ]
    for load in loads:
        load.start()

    def x_load(q):
        part = pl.ds(q * 16, 16)
        return pltpu.make_async_copy(x_hbm.at[part], x.at[part], x_sem.at[q])

    for q in range(4):
        x_load(q).start()

    barrier = pltpu.get_barrier_semaphore()

    def greet(k, to):
        pl.semaphore_signal(barrier, inc=1, device_id=to(k), device_id_type=MESH)

    others(row, lambda k: greet(k, on_row))
    others(col, lambda k: greet(k, on_col))

    mask[...] = one_hot(iota((256, 256), 0) // 32 == iota((256, 256), 1) // 32)
    m, n = iota((512, 128), 0), iota((512, 128), 1)
    fold[...] = one_hot((m // 128 == n // 32) & (m % 32 == n % 32))
    m, n = iota((16, 128), 0), iota((16, 128), 1)
    gather_s[...] = one_hot((m % 4 == n // 32) & (m // 4 == n % 32 // 8))
    same_block = iota((32, 128), 0) % 4 == iota((32, 128), 1) // 32
    same_dl = iota((128, 256), 0) % 8 == iota((128, 256), 1) // 32

    loads[0].wait()
    loads[1].wait()

    def unfolded(ref):
        parts = []
        for i in range(L):
            tiles = [
                jnp.broadcast_to(ref[pl.ds(i, 1), pl.ds(h * 128, 128)].astype(F32), (4, 128)) for h in range(8)
            ]
            parts.append(jnp.where(same_block, jnp.concatenate(tiles, axis=0), 0.0).astype(BF))
        return jnp.concatenate(parts, axis=1)

    own = dot(jnp.concatenate([unfolded(a_own), unfolded(b_own)], axis=0), fold[...])
    a_all[col] = own[0:32].astype(BF)
    spread_s = one_hot(iota((32, 256), 0) == iota((32, 256), 1) % 32)
    wide = jnp.where(same_dl, dot(own[32:64].T.astype(BF), spread_s), 0.0).astype(BF)
    b_all[row] = dot(gather_s[...], wide).astype(BF)

    loads[2].wait()
    loads[3].wait()
    w32[...] = w_own[...].astype(F32)
    for d in range(D):
        wp[pl.ds(d * C, C), :] = w32[pl.ds(d, C, stride=D), :].astype(BF)
    for q in range(8):
        wpt[:, pl.ds(q * 128, 128)] = wp[pl.ds(q * 128, 128), :].T

    def outer_grad(q):
        x_load(q).wait()
        rows = x[pl.ds(q * 16, 16)].reshape(16 * R, Z)
        part = dot(rows, wpt[...]).astype(BF)
        for dh in range(4):
            g[pl.ds(q * 16, 16), pl.ds(dh * R, R), :] = part[:, dh * 256 : dh * 256 + 256].reshape(16, R, 256)

    def x_transpose(q):
        for h in range(4):
            rows = x[pl.ds(q * 16 + h * 4, 4)].reshape(256, Z)
            xt[q, :, pl.ds(h * 256, 256)] = rows.T

    outer_grad(0)
    outer_grad(1)

    pl.semaphore_wait(barrier, 2 * (N - 1))
    others(row, lambda k: push(b_all.at[row], b_all.at[row], B, on_row(k)))
    others(col, lambda k: push(a_all.at[col], a_all.at[col], A, on_col(k)))

    outer_grad(2)
    outer_grad(3)
    for q in range(4):
        x_transpose(q)
    m, n = iota((128, 1024), 0), iota((128, 1024), 1)
    spread = jnp.where((m // 32 == n // 256) & (m % 32 == n % 32), SCALE, 0.0).astype(BF)

    wait_all(b_all, recv.at[B])
    bs32[...] = b_all[...].astype(F32)
    for q in range(N):
        for dh in range(4):
            b32[pl.ds(dh * R + q * L, L), :] = bs32[q, pl.ds(dh * L, L), :]
    bp[...] = b32[...].astype(BF)
    bpt[...] = b32[...].T.astype(BF)
    wait_all(a_all, recv.at[A])
    arep[...] = dot(a_all[...].reshape(N * S, 128), spread).astype(BF).reshape(N, S, 1024)
    for q in range(4):
        turned = a_all[pl.ds(q * 4, 4)].reshape(128, 128).T
        arept[q] = dot(turned, spread).astype(BF)

    def diagonal(block):
        return jnp.concatenate([block] * 8, axis=0) * mask[...]

    def outer(q, carry):
        for t in range(4):
            for i in range(L):
                rhs = diagonal(arep[q * 4 + t, :, pl.ds(i * 256, 256)])
                o[q * 16 + t * 4 + i] = dot(bp[...], rhs).astype(BF)
        return carry

    lax.fori_loop(0, 4, outer, 0)

    for dh in range(4):
        rows = [o[pl.ds(q * 16, 16), pl.ds(dh * R, R), :].reshape(16 * R, 256) for q in range(4)]
        part = dot(xt[0], rows[0]) + dot(xt[1], rows[1]) + dot(xt[2], rows[2]) + dot(xt[3], rows[3])
        for h in range(2):
            gwt[pl.ds(dh * 256 + h * 128, 128), :] = part[:, h * 128 : h * 128 + 128].T
        for k in (2 * dh, 2 * dh + 1, 2 * dh + 8, 2 * dh + 9):
            for dl in range(4):
                first = (4 * (k % 8) + dl) * C + k // 8
                w1_out[k, pl.ds(dl * 16, 16), :] = gwt[pl.ds(first, 16, stride=2), :].astype(BF)

            @pl.when(k != col)
            def _():
                push(w1_out.at[k], w1_in.at[col], W1, on_col(k))

    w1_in[col] = w1_out[col]

    for q in range(4):
        lhs = jnp.concatenate([g[q * 16 + i] for i in range(16)], axis=1)
        rhs = jnp.concatenate(
            [diagonal(arept[q, pl.ds(i % 4 * 32, 32), pl.ds(i // 4 * 256, 256)]) for i in range(16)], axis=0
        )
        if q == 0:
            gr[...] = dot(lhs, rhs)
        else:
            gr[...] += dot(lhs, rhs)
    for q in range(N):
        for dh in range(4):
            gs32[q, pl.ds(dh * L, L), :] = gr[pl.ds(dh * R + q * L, L), :]
    r_out[...] = gs32[...].astype(BF)
    r_in[row] = r_out[row]
    others(row, lambda k: push(r_out.at[k], r_in.at[row], GR, on_row(k)))

    lane4 = iota((32, 256), 1) % 128 // 32
    lane = iota((32, 128), 1) // 32

    def left_group(q):
        result = jnp.zeros((32, 128), F32)
        for two in range(2):
            i0 = q * L + two * 2
            both = jnp.zeros((32, 256), F32)
            for h in range(2):
                half = pl.ds(h * 128, 128)
                rhs = jnp.concatenate([g[i0, :, half], g[i0 + 1, :, half]], axis=1)
                part = dot(bpt[half, :], rhs)
                kept = part[96:128]
                for dl in range(3):
                    kept = jnp.where(lane4 == dl, part[dl * 32 : dl * 32 + 32], kept)
                both += kept
            for i in range(2):
                one = both[:, i * 128 : i * 128 + 128]
                one = one + pltpu.roll(one, 64, 1)
                one = one + pltpu.roll(one, 32, 1)
                result = jnp.where(lane == two * 2 + i, one, result)
        l_out[q] = result.astype(BF)

    def left_step(u, carry):
        for v in range(8):
            left_group(lax.rem(col + 8 * u + v + 1, N))
        for v in range(8):
            t = 8 * u + v + 1
            q = lax.rem(col + t, N)

            @pl.when(t < N)
            def _():
                push(l_out.at[q], l_in.at[col], GL, on_col(q))

        return carry

    lax.fori_loop(0, 2, left_step, 0)
    l_in[col] = l_out[col]

    wait_all(w1_in, recv.at[W1])
    total = w1_in[0].astype(F32)
    for k in range(1, N):
        total += w1_in[k].astype(F32)
    gwt[pl.ds(0, 64), :] = total
    for k in range(N):
        w2_out[k] = jnp.concatenate([gwt[pl.ds(k, 4, stride=16), :]] * 2, axis=0)
    w2_in[row] = w2_out[row]
    others(row, lambda k: push(w2_out.at[k], w2_in.at[row], W2, on_row(k)))

    for q in range(16):
        lhs = jnp.concatenate(
            [o[pl.ds(q * 4, 4), pl.ds(dh * R, R), :].reshape(4 * R, 256) for dh in range(4)], axis=1
        )
        total = dot(lhs, wp[...]) + bias[...]
        pair[pl.ds(q * 4, 4)] = total.astype(BF).reshape(4, R, Z)

    def folded(block):
        wide = lax.dot_general(block, fold[...], (((1,), (1,)), ((), ())), preferred_element_type=F32)
        kept = jnp.where(jnp.concatenate([same_block] * 4, axis=1), wide, 0.0).astype(BF)
        heads = one_hot(iota((8, 32), 0) == iota((8, 32), 1) // 4)
        tiles = dot(heads, kept)
        for i in range(L):
            for h in range(8):
                rows32[pl.ds(i, 1), pl.ds(h * 128, 128)] = tiles[h : h + 1, i * 128 : i * 128 + 128]
        return rows32[0:4, :].astype(BF)

    wait_all(r_in, recv.at[GR])
    total = r_in[0].astype(F32)
    for k in range(1, N):
        total += r_in[k].astype(F32)
    wide = lax.dot_general(
        gather_s[...], total.astype(BF), (((0,), (0,)), ((), ())), preferred_element_type=F32
    )
    wide = jnp.where(same_dl, wide, 0.0).astype(BF)
    by_s = lax.dot_general(spread_s, wide, (((1,), (1,)), ((), ())), preferred_element_type=F32)
    gr_ref[...] = folded(by_s.astype(BF))

    wait_all(l_in, recv.at[GL])
    total = l_in[0].astype(F32)
    for k in range(1, N):
        total += l_in[k].astype(F32)
    gl_ref[...] = folded((total * SCALE).astype(BF))

    wait_all(w2_in, recv.at[W2])
    total = w2_in[0]
    for k in range(1, N):
        total += w2_in[k]
    gw_ref[...] = total[0:4]

    for ref, which in ((a_all, A), (b_all, B), (w1_in, W1), (w2_in, W2), (l_in, GL), (r_in, GR)):
        wait_all(ref, send.at[which])


def store(pair, gl, gr, gw, pair_hbm, gl_hbm, gr_hbm, gw_hbm, sem):
    copies = [pltpu.make_async_copy(src, dst, sem.at[n]) for n, (src, dst) in enumerate(
        [(pair.at[pl.ds(q * 8, 8)], pair_hbm.at[pl.ds(q * 8, 8)]) for q in range(8)]
        + [(gl, gl_hbm), (gr, gr_hbm), (gw, gw_hbm)])]
    for copy in copies:
        copy.start()
    for copy in copies:
        copy.wait()


def shards(a, b, w, bias, x):
    vmem = pl.BlockSpec(memory_space=pltpu.VMEM)
    hbm = pl.BlockSpec(memory_space=pltpu.HBM)
    v = pltpu.VMEM
    outs = (
        jax.ShapeDtypeStruct((R, R, Z), BF),
        jax.ShapeDtypeStruct((L, S * C), BF),
        jax.ShapeDtypeStruct((L, S * D), BF),
        jax.ShapeDtypeStruct((4, Z), F32),
    )
    results = pl.pallas_call(
        kernel,
        out_shape=outs,
        in_specs=[hbm] * 5,
        out_specs=(vmem,) * 4,
        scratch_shapes=[
            v((L, 1024), BF), v((L, 1024), BF), v((1024, Z), BF), v((1, Z), F32),
            v((R, R, Z), BF), v((4, Z, 1024), BF), v((1024, Z), BF), v((Z, 1024), BF), v((1024, Z), F32),
            v((256, 256), BF), v((R, 256, 256), BF), v((R, 256, 256), BF),
            v((N, S, 1024), BF), v((4, 128, 1024), BF),
            v((256, 256), BF), v((256, 256), BF), v((256, 256), F32), v((N, 16, 256), F32),
            v((1024, Z), F32), v((256, 256), F32), v((N, 16, 256), F32),
            v((8, 1024), F32), v((512, 128), BF), v((16, 128), BF),
            v((N, S, 128), BF), v((N, 16, 256), BF),
            v((N, 64, Z), BF), v((N, 64, Z), BF), v((N, 8, Z), F32), v((N, 8, Z), F32),
            v((N, S, 128), BF), v((N, S, 128), BF), v((N, 16, 256), BF), v((N, 16, 256), BF),
            pltpu.SemaphoreType.DMA((4,)), pltpu.SemaphoreType.DMA((4,)),
            pltpu.SemaphoreType.DMA((6,)), pltpu.SemaphoreType.DMA((6,)),
        ],
        compiler_params=pltpu.CompilerParams(
            collective_id=0, has_side_effects=True, vmem_limit_bytes=48 * 2**20
        ),
        cost_estimate=pl.CostEstimate(
            flops=8_000_000_000, bytes_accessed=3_000_000, transcendentals=0
        ),
    )(*[pltpu.with_memory_space_constraint(t, pltpu.HBM) for t in (a, b, w, bias.reshape(1, Z), x)])
    return pl.pallas_call(
        store,
        out_shape=outs,
        in_specs=[vmem] * 4,
        out_specs=(hbm,) * 4,
        scratch_shapes=[pltpu.SemaphoreType.DMA((11,))],
    )(*results)


def solution(mesh):
    in_specs = (P(("row", "col"), None), P(("col", "row"), None), P(), P(), P("row", "col", None))
    out_specs = (
        P("row", "col", None),
        P(("row", "col"), None),
        P(("col", "row"), None),
        P(("row", "col"), None),
    )
    return jax.shard_map(shards, mesh=mesh, in_specs=in_specs, out_specs=out_specs, check_vma=False)
```

```python
import jax
import jax.numpy as jnp
from jax import lax
from jax.experimental import pallas as pl
from jax.experimental.pallas import tpu as pltpu
from jax.sharding import PartitionSpec as P

MESH = pl.DeviceIdType.MESH
BF, F32 = jnp.bfloat16, jnp.float32
S, C, D, Z = 32, 32, 32, 128
N = 16
L = 4
R = N * L
SCALE = 1.0 / S


def dot(a, b):
    return jnp.dot(a, b, preferred_element_type=F32)


def iota(shape, dim):
    return lax.broadcasted_iota(jnp.int32, shape, dim)


def one_hot(condition):
    return jnp.where(condition, 1.0, 0.0).astype(BF)


def kernel(
    a_hbm, b_hbm, w_hbm, bias_hbm, x_hbm, pair, gl_ref, gr_ref, gw_ref,
    a_own, b_own, w_own, bias, x, xt, wp, wpt, w32, mask, g, o, arep, arept, bp, bpt, b32, bs32,
    gwt, gr, gs32, rows32, fold, gather_s,
    a_all, b_all, w1_out, w1_in, w2_out, w2_in, l_out, l_in, r_out, r_in,
    own_sem, x_sem, send, recv,
):
    row, col = lax.axis_index("row"), lax.axis_index("col")

    y, z = row // 4, lax.rem(row, 4)
    u, zl, core = col // 4, lax.rem(col // 2, 2), lax.rem(col, 2)
    around, apart = (0, 1, 2, 1), (0, 2, 4, 2)
    row_steps = sorted(
        ((dy, dz) for dy in range(4) for dz in range(4) if dy or dz), key=lambda t: -around[t[0]] - apart[t[1]]
    )
    col_steps = sorted(
        ((dx, dz, dc) for dx in range(4) for dz in range(2) for dc in range(2) if dx or dz or dc),
        key=lambda t: -around[t[0]] - t[1],
    )
    row_peers = [lax.rem(y + dy, 4) * 4 + lax.rem(z + dz, 4) for dy, dz in row_steps]
    col_peers = [
        lax.rem(u + dx, 4) * 4 + lax.rem(zl + dz, 2) * 2 + lax.rem(core + dc, 2) for dx, dz, dc in col_steps
    ]

    def on_col(k):
        return (row, k)

    def on_row(k):
        return (k, col)

    def push(src, dst, which, device):
        pltpu.make_async_remote_copy(
            src_ref=src, dst_ref=dst, send_sem=send.at[which], recv_sem=recv.at[which],
            device_id=device, device_id_type=MESH,
        ).start()

    def others(peers, body):
        for k in peers:
            body(k)

    def wait_all(ref, sem):
        blocks = ref.at[pl.ds(0, N - 1)]
        pltpu.make_async_copy(blocks, blocks, sem).wait()

    A, B, W1, W2, GL, GR = range(6)

    loads = [
        pltpu.make_async_copy(src, dst, own_sem.at[n])
        for n, (src, dst) in enumerate(((a_hbm, a_own), (b_hbm, b_own), (w_hbm, w_own), (bias_hbm, bias)))
    ]
    for load in loads:
        load.start()

    def x_load(q):
        part = pl.ds(q * 16, 16)
        return pltpu.make_async_copy(x_hbm.at[part], x.at[part], x_sem.at[q])

    for q in range(4):
        x_load(q).start()

    barrier = pltpu.get_barrier_semaphore()

    def greet(k, to):
        pl.semaphore_signal(barrier, inc=1, device_id=to(k), device_id_type=MESH)

    others(row_peers, lambda k: greet(k, on_row))
    others(col_peers, lambda k: greet(k, on_col))

    mask[...] = one_hot(iota((256, 256), 0) // 32 == iota((256, 256), 1) // 32)
    m, n = iota((512, 128), 0), iota((512, 128), 1)
    fold[...] = one_hot((m // 128 == n // 32) & (m % 32 == n % 32))
    m, n = iota((16, 128), 0), iota((16, 128), 1)
    gather_s[...] = one_hot((m % 4 == n // 32) & (m // 4 == n % 32 // 8))
    same_block = iota((32, 128), 0) % 4 == iota((32, 128), 1) // 32
    same_dl = iota((128, 256), 0) % 8 == iota((128, 256), 1) // 32

    loads[0].wait()
    loads[1].wait()

    def unfolded(ref):
        parts = []
        for i in range(L):
            tiles = [
                jnp.broadcast_to(ref[pl.ds(i, 1), pl.ds(h * 128, 128)].astype(F32), (4, 128)) for h in range(8)
            ]
            parts.append(jnp.where(same_block, jnp.concatenate(tiles, axis=0), 0.0).astype(BF))
        return jnp.concatenate(parts, axis=1)

    own = dot(jnp.concatenate([unfolded(a_own), unfolded(b_own)], axis=0), fold[...])
    a_all[col] = own[0:32].astype(BF)
    spread_s = one_hot(iota((32, 256), 0) == iota((32, 256), 1) % 32)
    wide = jnp.where(same_dl, dot(own[32:64].T.astype(BF), spread_s), 0.0).astype(BF)
    b_all[row] = dot(gather_s[...], wide).astype(BF)

    loads[2].wait()
    loads[3].wait()
    w32[...] = w_own[...].astype(F32)
    for d in range(D):
        wp[pl.ds(d * C, C), :] = w32[pl.ds(d, C, stride=D), :].astype(BF)
    for q in range(8):
        wpt[:, pl.ds(q * 128, 128)] = wp[pl.ds(q * 128, 128), :].T

    def outer_grad(q):
        x_load(q).wait()
        rows = x[pl.ds(q * 16, 16)].reshape(16 * R, Z)
        part = dot(rows, wpt[...]).astype(BF)
        for dh in range(4):
            g[pl.ds(q * 16, 16), pl.ds(dh * R, R), :] = part[:, dh * 256 : dh * 256 + 256].reshape(16, R, 256)

    def x_transpose(q):
        for h in range(4):
            rows = x[pl.ds(q * 16 + h * 4, 4)].reshape(256, Z)
            xt[q, :, pl.ds(h * 256, 256)] = rows.T

    outer_grad(0)
    outer_grad(1)

    pl.semaphore_wait(barrier, 2 * (N - 1))
    others(row_peers, lambda k: push(b_all.at[row], b_all.at[row], B, on_row(k)))
    others(col_peers, lambda k: push(a_all.at[col], a_all.at[col], A, on_col(k)))

    outer_grad(2)
    outer_grad(3)
    for q in range(4):
        x_transpose(q)
    m, n = iota((128, 1024), 0), iota((128, 1024), 1)
    spread = jnp.where((m // 32 == n // 256) & (m % 32 == n % 32), SCALE, 0.0).astype(BF)

    wait_all(a_all, recv.at[A])
    arep[...] = dot(a_all[...].reshape(N * S, 128), spread).astype(BF).reshape(N, S, 1024)
    for q in range(4):
        turned = a_all[pl.ds(q * 4, 4)].reshape(128, 128).T
        arept[q] = dot(turned, spread).astype(BF)

    def diagonal(block):
        return jnp.concatenate([block] * 8, axis=0) * mask[...]

    for q in range(4):
        lhs = jnp.concatenate([g[q * 16 + i] for i in range(16)], axis=1)
        rhs = jnp.concatenate(
            [diagonal(arept[q, pl.ds(i % 4 * 32, 32), pl.ds(i // 4 * 256, 256)]) for i in range(16)], axis=0
        )
        if q == 0:
            gr[...] = dot(lhs, rhs)
        else:
            gr[...] += dot(lhs, rhs)
    for q in range(N):
        for dh in range(4):
            gs32[q, pl.ds(dh * L, L), :] = gr[pl.ds(dh * R + q * L, L), :]
    r_out[...] = gs32[...].astype(BF)
    r_in[row] = r_out[row]
    others(row_peers, lambda k: push(r_out.at[k], r_in.at[row], GR, on_row(k)))

    wait_all(b_all, recv.at[B])
    bs32[...] = b_all[...].astype(F32)
    for q in range(N):
        for dh in range(4):
            b32[pl.ds(dh * R + q * L, L), :] = bs32[q, pl.ds(dh * L, L), :]
    bp[...] = b32[...].astype(BF)
    bpt[...] = b32[...].T.astype(BF)
    def outer(q, carry):
        for t in range(8):
            for i in range(L):
                rhs = diagonal(arep[q * 8 + t, :, pl.ds(i * 256, 256)])
                o[q * 32 + t * 4 + i] = dot(bp[...], rhs).astype(BF)
        return carry

    lax.fori_loop(0, 2, outer, 0)

    side = lax.rem(u, 2)
    for sx, sz in ((0, 1), (0, 0), (1, 1), (1, 0)):
        x1, z1 = lax.rem(side + sx, 2), lax.rem(zl + sz, 2)
        dh = x1 * 2 + z1
        rows = [o[pl.ds(q * 16, 16), pl.ds(dh * R, R), :].reshape(16 * R, 256) for q in range(4)]
        part = dot(xt[0], rows[0]) + dot(xt[1], rows[1]) + dot(xt[2], rows[2]) + dot(xt[3], rows[3])
        for h in range(2):
            gwt[pl.ds(h * 128, 128), :] = part[:, h * 128 : h * 128 + 128].T
        for up in (1, 0):
            for c1 in range(2):
                first_x = lax.rem(u + 2 * up, 4) if sx == 0 else x1 + 2 * up
                k = first_x * 4 + z1 * 2 + c1
                for dl in range(4):
                    first = (4 * c1 + dl) * C + first_x // 2
                    w1_out[k, pl.ds(dl * 16, 16), :] = gwt[pl.ds(first, 16, stride=2), :].astype(BF)

                @pl.when(k != col)
                def _():
                    push(w1_out.at[k], w1_in.at[col], W1, on_col(k))

    w1_in[col] = w1_out[col]

    lane4 = iota((32, 256), 1) % 128 // 32
    lane = iota((32, 128), 1) // 32

    def left_group(q):
        result = jnp.zeros((32, 128), F32)
        for two in range(2):
            i0 = q * L + two * 2
            both = jnp.zeros((32, 256), F32)
            for h in range(2):
                half = pl.ds(h * 128, 128)
                rhs = jnp.concatenate([g[i0, :, half], g[i0 + 1, :, half]], axis=1)
                part = dot(bpt[half, :], rhs)
                kept = part[96:128]
                for dl in range(3):
                    kept = jnp.where(lane4 == dl, part[dl * 32 : dl * 32 + 32], kept)
                both += kept
            for i in range(2):
                one = both[:, i * 128 : i * 128 + 128]
                one = one + pltpu.roll(one, 64, 1)
                one = one + pltpu.roll(one, 32, 1)
                result = jnp.where(lane == two * 2 + i, one, result)
        l_out[q] = result.astype(BF)

    def left_step(u, carry):
        for v in range(8):
            left_group(lax.rem(col + 8 * u + v + 1, N))
        for v in range(8):
            t = 8 * u + v + 1
            q = lax.rem(col + t, N)

            @pl.when(t < N)
            def _():
                push(l_out.at[q], l_in.at[col], GL, on_col(q))

        return carry

    lax.fori_loop(0, 2, left_step, 0)
    l_in[col] = l_out[col]

    def pair_blocks(blocks):
        for q in blocks:
            lhs = jnp.concatenate(
                [o[pl.ds(q * 4, 4), pl.ds(dh * R, R), :].reshape(4 * R, 256) for dh in range(4)], axis=1
            )
            total = dot(lhs, wp[...]) + bias[...]
            pair[pl.ds(q * 4, 4)] = total.astype(BF).reshape(4, R, Z)

    pair_blocks(range(8))

    wait_all(w1_in, recv.at[W1])
    total = w1_in[0].astype(F32)
    for k in range(1, N):
        total += w1_in[k].astype(F32)
    gwt[pl.ds(0, 64), :] = total
    for k in range(N):
        w2_out[k] = gwt[pl.ds(k, 4, stride=16), :]
    w2_in[row] = w2_out[row]
    others(row_peers, lambda k: push(w2_out.at[k], w2_in.at[row], W2, on_row(k)))

    pair_blocks(range(8, 16))

    def folded(block):
        wide = lax.dot_general(block, fold[...], (((1,), (1,)), ((), ())), preferred_element_type=F32)
        kept = jnp.where(jnp.concatenate([same_block] * 4, axis=1), wide, 0.0).astype(BF)
        heads = one_hot(iota((8, 32), 0) == iota((8, 32), 1) // 4)
        tiles = dot(heads, kept)
        for i in range(L):
            for h in range(8):
                rows32[pl.ds(i, 1), pl.ds(h * 128, 128)] = tiles[h : h + 1, i * 128 : i * 128 + 128]
        return rows32[0:4, :].astype(BF)

    wait_all(r_in, recv.at[GR])
    total = r_in[0].astype(F32)
    for k in range(1, N):
        total += r_in[k].astype(F32)
    wide = lax.dot_general(
        gather_s[...], total.astype(BF), (((0,), (0,)), ((), ())), preferred_element_type=F32
    )
    wide = jnp.where(same_dl, wide, 0.0).astype(BF)
    by_s = lax.dot_general(spread_s, wide, (((1,), (1,)), ((), ())), preferred_element_type=F32)
    gr_ref[...] = folded(by_s.astype(BF))

    wait_all(l_in, recv.at[GL])
    total = l_in[0].astype(F32)
    for k in range(1, N):
        total += l_in[k].astype(F32)
    gl_ref[...] = folded((total * SCALE).astype(BF))

    for ref, which in ((a_all, A), (b_all, B), (w1_in, W1), (l_in, GL), (r_in, GR), (w2_in, W2)):
        wait_all(ref, send.at[which])

    wait_all(w2_in, recv.at[W2])
    total = w2_in[0]
    for k in range(1, N):
        total += w2_in[k]
    gw_ref[...] = total


def store(pair, gl, gr, gw, pair_hbm, gl_hbm, gr_hbm, gw_hbm, sem):
    copies = [pltpu.make_async_copy(src, dst, sem.at[n]) for n, (src, dst) in enumerate(
        [(pair.at[pl.ds(q * 8, 8)], pair_hbm.at[pl.ds(q * 8, 8)]) for q in range(8)]
        + [(gl, gl_hbm), (gr, gr_hbm), (gw, gw_hbm)])]
    for copy in copies:
        copy.start()
    for copy in copies:
        copy.wait()


def shards(a, b, w, bias, x):
    vmem = pl.BlockSpec(memory_space=pltpu.VMEM)
    hbm = pl.BlockSpec(memory_space=pltpu.HBM)
    v = pltpu.VMEM
    outs = (
        jax.ShapeDtypeStruct((R, R, Z), BF),
        jax.ShapeDtypeStruct((L, S * C), BF),
        jax.ShapeDtypeStruct((L, S * D), BF),
        jax.ShapeDtypeStruct((4, Z), F32),
    )
    results = pl.pallas_call(
        kernel,
        out_shape=outs,
        in_specs=[hbm] * 5,
        out_specs=(vmem,) * 4,
        scratch_shapes=[
            v((L, 1024), BF), v((L, 1024), BF), v((1024, Z), BF), v((1, Z), F32),
            v((R, R, Z), BF), v((4, Z, 1024), BF), v((1024, Z), BF), v((Z, 1024), BF), v((1024, Z), F32),
            v((256, 256), BF), v((R, 256, 256), BF), v((R, 256, 256), BF),
            v((N, S, 1024), BF), v((4, 128, 1024), BF),
            v((256, 256), BF), v((256, 256), BF), v((256, 256), F32), v((N, 16, 256), F32),
            v((256, Z), F32), v((256, 256), F32), v((N, 16, 256), F32),
            v((8, 1024), F32), v((512, 128), BF), v((16, 128), BF),
            v((N, S, 128), BF), v((N, 16, 256), BF),
            v((N, 64, Z), BF), v((N, 64, Z), BF), v((N, 4, Z), F32), v((N, 4, Z), F32),
            v((N, S, 128), BF), v((N, S, 128), BF), v((N, 16, 256), BF), v((N, 16, 256), BF),
            pltpu.SemaphoreType.DMA((4,)), pltpu.SemaphoreType.DMA((4,)),
            pltpu.SemaphoreType.DMA((6,)), pltpu.SemaphoreType.DMA((6,)),
        ],
        compiler_params=pltpu.CompilerParams(
            collective_id=0, has_side_effects=True, vmem_limit_bytes=48 * 2**20
        ),
        cost_estimate=pl.CostEstimate(
            flops=8_000_000_000, bytes_accessed=3_000_000, transcendentals=0
        ),
    )(*[pltpu.with_memory_space_constraint(t, pltpu.HBM) for t in (a, b, w, bias.reshape(1, Z), x)])
    return pl.pallas_call(
        store,
        out_shape=outs,
        in_specs=[vmem] * 4,
        out_specs=(hbm,) * 4,
        scratch_shapes=[pltpu.SemaphoreType.DMA((11,))],
        compiler_params=pltpu.CompilerParams(vmem_limit_bytes=2**20),
    )(*[pltpu.with_memory_space_constraint(t, pltpu.VMEM) for t in results])


def solution(mesh):
    in_specs = (P(("row", "col"), None), P(("col", "row"), None), P(), P(), P("row", "col", None))
    out_specs = (
        P("row", "col", None),
        P(("row", "col"), None),
        P(("col", "row"), None),
        P(("row", "col"), None),
    )
    return jax.shard_map(shards, mesh=mesh, in_specs=in_specs, out_specs=out_specs, check_vma=False)
```

```python
import jax
import jax.numpy as jnp
from jax import lax
from jax.experimental import pallas as pl
from jax.experimental.pallas import tpu as pltpu
from jax.sharding import PartitionSpec as P

MESH = pl.DeviceIdType.MESH
BF, F32 = jnp.bfloat16, jnp.float32
S, C, D, Z = 32, 32, 32, 128
N = 16
L = 4
R = N * L
SCALE = 1.0 / S


def dot(a, b):
    return jnp.dot(a, b, preferred_element_type=F32)


def iota(shape, dim):
    return lax.broadcasted_iota(jnp.int32, shape, dim)


def one_hot(condition):
    return jnp.where(condition, 1.0, 0.0).astype(BF)


def kernel(
    a_hbm, b_hbm, w_hbm, bias_hbm, x_hbm, pair, gl_ref, gr_ref, gw_ref,
    a_own, b_own, w_own, bias, x, xt, wp, wpt, w32, mask, g, o, arep, arept, bp, bpt, b32, bs32,
    gwt, gr, gs32, rows32, fold, gather_s,
    a_all, b_all, w1_out, w1_in, w2_out, w2_in, l_out, l_in, r_out, r_in,
    own_sem, x_sem, send, recv,
):
    row, col = lax.axis_index("row"), lax.axis_index("col")

    y, z = row // 4, lax.rem(row, 4)
    u, zl, core = col // 4, lax.rem(col // 2, 2), lax.rem(col, 2)
    around, apart = (0, 1, 2, 1), (0, 2, 4, 2)
    row_steps = sorted(
        ((dy, dz) for dy in range(4) for dz in range(4) if dy or dz), key=lambda t: -around[t[0]] - apart[t[1]]
    )
    col_steps = sorted(
        ((dx, dz, dc) for dx in range(4) for dz in range(2) for dc in range(2) if dx or dz or dc),
        key=lambda t: -around[t[0]] - t[1],
    )
    row_peers = [lax.rem(y + dy, 4) * 4 + lax.rem(z + dz, 4) for dy, dz in row_steps]
    col_peers = [
        lax.rem(u + dx, 4) * 4 + lax.rem(zl + dz, 2) * 2 + lax.rem(core + dc, 2) for dx, dz, dc in col_steps
    ]

    def on_col(k):
        return (row, k)

    def on_row(k):
        return (k, col)

    def push(src, dst, which, device):
        pltpu.make_async_remote_copy(
            src_ref=src, dst_ref=dst, send_sem=send.at[which], recv_sem=recv.at[which],
            device_id=device, device_id_type=MESH,
        ).start()

    def others(peers, body):
        for k in peers:
            body(k)

    def wait_all(ref, sem):
        blocks = ref.at[pl.ds(0, N - 1)]
        pltpu.make_async_copy(blocks, blocks, sem).wait()

    A, B, W1, W2, GL, GR = range(6)

    loads = [
        pltpu.make_async_copy(src, dst, own_sem.at[n])
        for n, (src, dst) in enumerate(((a_hbm, a_own), (b_hbm, b_own), (w_hbm, w_own), (bias_hbm, bias)))
    ]
    for load in loads:
        load.start()

    barrier = pltpu.get_barrier_semaphore()

    def greet(k, to):
        pl.semaphore_signal(barrier, inc=1, device_id=to(k), device_id_type=MESH)

    others(row_peers, lambda k: greet(k, on_row))
    others(col_peers, lambda k: greet(k, on_col))

    def x_load(q):
        part = pl.ds(q * 16, 16)
        return pltpu.make_async_copy(x_hbm.at[part], x.at[part], x_sem.at[q])

    for q in range(4):
        x_load(q).start()

    mask[...] = one_hot(iota((256, 256), 0) // 32 == iota((256, 256), 1) // 32)
    m, n = iota((512, 128), 0), iota((512, 128), 1)
    fold[...] = one_hot((m // 128 == n // 32) & (m % 32 == n % 32))
    m, n = iota((16, 128), 0), iota((16, 128), 1)
    gather_s[...] = one_hot((m % 4 == n // 32) & (m // 4 == n % 32 // 8))
    same_block = iota((32, 128), 0) % 4 == iota((32, 128), 1) // 32
    same_dl = iota((128, 256), 0) % 8 == iota((128, 256), 1) // 32

    loads[0].wait()
    loads[1].wait()

    def unfolded(ref):
        parts = []
        for i in range(L):
            tiles = [
                jnp.broadcast_to(ref[pl.ds(i, 1), pl.ds(h * 128, 128)].astype(F32), (4, 128)) for h in range(8)
            ]
            parts.append(jnp.where(same_block, jnp.concatenate(tiles, axis=0), 0.0).astype(BF))
        return jnp.concatenate(parts, axis=1)

    own = dot(jnp.concatenate([unfolded(a_own), unfolded(b_own)], axis=0), fold[...])
    a_all[col] = own[0:32].astype(BF)
    spread_s = one_hot(iota((32, 256), 0) == iota((32, 256), 1) % 32)
    wide = jnp.where(same_dl, dot(own[32:64].T.astype(BF), spread_s), 0.0).astype(BF)
    b_all[row] = dot(gather_s[...], wide).astype(BF)

    pl.semaphore_wait(barrier, 2 * (N - 1))
    others(row_peers, lambda k: push(b_all.at[row], b_all.at[row], B, on_row(k)))
    others(col_peers, lambda k: push(a_all.at[col], a_all.at[col], A, on_col(k)))

    loads[2].wait()
    loads[3].wait()
    w32[...] = w_own[...].astype(F32)
    for d in range(D):
        wp[pl.ds(d * C, C), :] = w32[pl.ds(d, C, stride=D), :].astype(BF)
    for q in range(8):
        wpt[:, pl.ds(q * 128, 128)] = wp[pl.ds(q * 128, 128), :].T

    def outer_grad(q):
        x_load(q).wait()
        rows = x[pl.ds(q * 16, 16)].reshape(16 * R, Z)
        part = dot(rows, wpt[...]).astype(BF)
        for dh in range(4):
            g[pl.ds(q * 16, 16), pl.ds(dh * R, R), :] = part[:, dh * 256 : dh * 256 + 256].reshape(16, R, 256)

    def x_transpose(q):
        for h in range(4):
            rows = x[pl.ds(q * 16 + h * 4, 4)].reshape(256, Z)
            xt[q, :, pl.ds(h * 256, 256)] = rows.T

    for q in range(4):
        outer_grad(q)
    for q in range(4):
        x_transpose(q)
    m, n = iota((128, 1024), 0), iota((128, 1024), 1)
    spread = jnp.where((m // 32 == n // 256) & (m % 32 == n % 32), SCALE, 0.0).astype(BF)

    wait_all(a_all, recv.at[A])
    arep[...] = dot(a_all[...].reshape(N * S, 128), spread).astype(BF).reshape(N, S, 1024)
    for q in range(4):
        turned = a_all[pl.ds(q * 4, 4)].reshape(128, 128).T
        arept[q] = dot(turned, spread).astype(BF)

    def diagonal(block):
        return jnp.concatenate([block] * 8, axis=0) * mask[...]

    gr[...] = jnp.zeros_like(gr)

    def right_grad(step, carry):
        for v in range(2):
            q = step * 2 + v
            lhs = jnp.concatenate([g[q * 16 + i] for i in range(16)], axis=1)
            rhs = jnp.concatenate(
                [diagonal(arept[q, pl.ds(i % 4 * 32, 32), pl.ds(i // 4 * 256, 256)]) for i in range(16)], axis=0
            )
            gr[...] += dot(lhs, rhs)
        return carry

    lax.fori_loop(0, 2, right_grad, 0)
    for q in range(N):
        for dh in range(4):
            gs32[q, pl.ds(dh * L, L), :] = gr[pl.ds(dh * R + q * L, L), :]
    r_out[...] = gs32[...].astype(BF)
    r_in[row] = r_out[row]
    others(row_peers, lambda k: push(r_out.at[k], r_in.at[row], GR, on_row(k)))

    wait_all(b_all, recv.at[B])
    bs32[...] = b_all[...].astype(F32)
    for q in range(N):
        for dh in range(4):
            b32[pl.ds(dh * R + q * L, L), :] = bs32[q, pl.ds(dh * L, L), :]
    bp[...] = b32[...].astype(BF)
    bpt[...] = b32[...].T.astype(BF)
    def outer(q, carry):
        for t in range(8):
            for i in range(L):
                rhs = diagonal(arep[q * 8 + t, :, pl.ds(i * 256, 256)])
                o[q * 32 + t * 4 + i] = dot(bp[...], rhs).astype(BF)
        return carry

    lax.fori_loop(0, 2, outer, 0)

    side = lax.rem(u, 2)
    for sx, sz in ((0, 1), (0, 0), (1, 1), (1, 0)):
        x1, z1 = lax.rem(side + sx, 2), lax.rem(zl + sz, 2)
        dh = x1 * 2 + z1
        rows = [o[pl.ds(q * 16, 16), pl.ds(dh * R, R), :].reshape(16 * R, 256) for q in range(4)]
        part = dot(xt[0], rows[0]) + dot(xt[1], rows[1]) + dot(xt[2], rows[2]) + dot(xt[3], rows[3])
        for h in range(2):
            gwt[pl.ds(h * 128, 128), :] = part[:, h * 128 : h * 128 + 128].T
        for up in (1, 0):
            for c1 in range(2):
                first_x = lax.rem(u + 2 * up, 4) if sx == 0 else x1 + 2 * up
                k = first_x * 4 + z1 * 2 + c1
                for dl in range(4):
                    first = (4 * c1 + dl) * C + first_x // 2
                    w1_out[k, pl.ds(dl * 16, 16), :] = gwt[pl.ds(first, 16, stride=2), :].astype(BF)

                @pl.when(k != col)
                def _():
                    push(w1_out.at[k], w1_in.at[col], W1, on_col(k))

    w1_in[col] = w1_out[col]

    lane4 = iota((32, 256), 1) % 128 // 32
    lane = iota((32, 128), 1) // 32

    def left_group(q):
        result = jnp.zeros((32, 128), F32)
        for two in range(2):
            i0 = q * L + two * 2
            both = jnp.zeros((32, 256), F32)
            for h in range(2):
                half = pl.ds(h * 128, 128)
                rhs = jnp.concatenate([g[i0, :, half], g[i0 + 1, :, half]], axis=1)
                part = dot(bpt[half, :], rhs)
                kept = part[96:128]
                for dl in range(3):
                    kept = jnp.where(lane4 == dl, part[dl * 32 : dl * 32 + 32], kept)
                both += kept
            for i in range(2):
                one = both[:, i * 128 : i * 128 + 128]
                one = one + pltpu.roll(one, 64, 1)
                one = one + pltpu.roll(one, 32, 1)
                result = jnp.where(lane == two * 2 + i, one, result)
        l_out[q] = result.astype(BF)

    def left_step(u, carry):
        for v in range(8):
            left_group(lax.rem(col + 8 * u + v + 1, N))
        for v in range(8):
            t = 8 * u + v + 1
            q = lax.rem(col + t, N)

            @pl.when(t < N)
            def _():
                push(l_out.at[q], l_in.at[col], GL, on_col(q))

        return carry

    lax.fori_loop(0, 2, left_step, 0)
    l_in[col] = l_out[col]

    def pair_blocks(blocks):
        for q in blocks:
            lhs = jnp.concatenate(
                [o[pl.ds(q * 4, 4), pl.ds(dh * R, R), :].reshape(4 * R, 256) for dh in range(4)], axis=1
            )
            total = dot(lhs, wp[...]) + bias[...]
            pair[pl.ds(q * 4, 4)] = total.astype(BF).reshape(4, R, Z)

    pair_blocks(range(8))

    wait_all(w1_in, recv.at[W1])
    total = w1_in[0].astype(F32)
    for k in range(1, N):
        total += w1_in[k].astype(F32)
    gwt[pl.ds(0, 64), :] = total
    for k in range(N):
        w2_out[k] = gwt[pl.ds(k, 4, stride=16), :]
    w2_in[row] = w2_out[row]
    others(row_peers, lambda k: push(w2_out.at[k], w2_in.at[row], W2, on_row(k)))

    pair_blocks(range(8, 16))

    def folded(block):
        wide = lax.dot_general(block, fold[...], (((1,), (1,)), ((), ())), preferred_element_type=F32)
        kept = jnp.where(jnp.concatenate([same_block] * 4, axis=1), wide, 0.0).astype(BF)
        heads = one_hot(iota((8, 32), 0) == iota((8, 32), 1) // 4)
        tiles = dot(heads, kept)
        for i in range(L):
            for h in range(8):
                rows32[pl.ds(i, 1), pl.ds(h * 128, 128)] = tiles[h : h + 1, i * 128 : i * 128 + 128]
        return rows32[0:4, :].astype(BF)

    wait_all(r_in, recv.at[GR])
    total = r_in[0].astype(F32)
    for k in range(1, N):
        total += r_in[k].astype(F32)
    wide = lax.dot_general(
        gather_s[...], total.astype(BF), (((0,), (0,)), ((), ())), preferred_element_type=F32
    )
    wide = jnp.where(same_dl, wide, 0.0).astype(BF)
    by_s = lax.dot_general(spread_s, wide, (((1,), (1,)), ((), ())), preferred_element_type=F32)
    gr_ref[...] = folded(by_s.astype(BF))

    wait_all(l_in, recv.at[GL])
    total = l_in[0].astype(F32)
    for k in range(1, N):
        total += l_in[k].astype(F32)
    gl_ref[...] = folded((total * SCALE).astype(BF))

    for ref, which in ((a_all, A), (b_all, B), (w1_in, W1), (l_in, GL), (r_in, GR), (w2_in, W2)):
        wait_all(ref, send.at[which])

    wait_all(w2_in, recv.at[W2])
    total = w2_in[0]
    for k in range(1, N):
        total += w2_in[k]
    gw_ref[...] = total


def store(pair, gl, gr, gw, pair_hbm, gl_hbm, gr_hbm, gw_hbm, sem):
    copies = [pltpu.make_async_copy(src, dst, sem.at[n]) for n, (src, dst) in enumerate(
        [(pair.at[pl.ds(q * 8, 8)], pair_hbm.at[pl.ds(q * 8, 8)]) for q in range(8)]
        + [(gl, gl_hbm), (gr, gr_hbm), (gw, gw_hbm)])]
    for copy in copies:
        copy.start()
    for copy in copies:
        copy.wait()


def shards(a, b, w, bias, x):
    vmem = pl.BlockSpec(memory_space=pltpu.VMEM)
    hbm = pl.BlockSpec(memory_space=pltpu.HBM)
    v = pltpu.VMEM
    outs = (
        jax.ShapeDtypeStruct((R, R, Z), BF),
        jax.ShapeDtypeStruct((L, S * C), BF),
        jax.ShapeDtypeStruct((L, S * D), BF),
        jax.ShapeDtypeStruct((4, Z), F32),
    )
    results = pl.pallas_call(
        kernel,
        out_shape=outs,
        in_specs=[hbm] * 5,
        out_specs=(vmem,) * 4,
        scratch_shapes=[
            v((L, 1024), BF), v((L, 1024), BF), v((1024, Z), BF), v((1, Z), F32),
            v((R, R, Z), BF), v((4, Z, 1024), BF), v((1024, Z), BF), v((Z, 1024), BF), v((1024, Z), F32),
            v((256, 256), BF), v((R, 256, 256), BF), v((R, 256, 256), BF),
            v((N, S, 1024), BF), v((4, 128, 1024), BF),
            v((256, 256), BF), v((256, 256), BF), v((256, 256), F32), v((N, 16, 256), F32),
            v((256, Z), F32), v((256, 256), F32), v((N, 16, 256), F32),
            v((8, 1024), F32), v((512, 128), BF), v((16, 128), BF),
            v((N, S, 128), BF), v((N, 16, 256), BF),
            v((N, 64, Z), BF), v((N, 64, Z), BF), v((N, 4, Z), F32), v((N, 4, Z), F32),
            v((N, S, 128), BF), v((N, S, 128), BF), v((N, 16, 256), BF), v((N, 16, 256), BF),
            pltpu.SemaphoreType.DMA((4,)), pltpu.SemaphoreType.DMA((4,)),
            pltpu.SemaphoreType.DMA((6,)), pltpu.SemaphoreType.DMA((6,)),
        ],
        compiler_params=pltpu.CompilerParams(
            collective_id=0, has_side_effects=True, vmem_limit_bytes=48 * 2**20
        ),
        cost_estimate=pl.CostEstimate(
            flops=8_000_000_000, bytes_accessed=3_000_000, transcendentals=0
        ),
    )(*[pltpu.with_memory_space_constraint(t, pltpu.HBM) for t in (a, b, w, bias.reshape(1, Z), x)])
    return pl.pallas_call(
        store,
        out_shape=outs,
        in_specs=[vmem] * 4,
        out_specs=(hbm,) * 4,
        scratch_shapes=[pltpu.SemaphoreType.DMA((11,))],
        compiler_params=pltpu.CompilerParams(vmem_limit_bytes=2**20),
    )(*[pltpu.with_memory_space_constraint(t, pltpu.VMEM) for t in results])


def solution(mesh):
    in_specs = (P(("row", "col"), None), P(("col", "row"), None), P(), P(), P("row", "col", None))
    out_specs = (
        P("row", "col", None),
        P(("row", "col"), None),
        P(("col", "row"), None),
        P(("row", "col"), None),
    )
    return jax.shard_map(shards, mesh=mesh, in_specs=in_specs, out_specs=out_specs, check_vma=False)
```

```python
import jax
import jax.numpy as jnp
from jax import lax
from jax.experimental import pallas as pl
from jax.experimental.pallas import tpu as pltpu
from jax.sharding import PartitionSpec as P

MESH = pl.DeviceIdType.MESH
BF, F32 = jnp.bfloat16, jnp.float32
S, C, D, Z = 32, 32, 32, 128
N = 16
L = 4
R = N * L
SCALE = 1.0 / S


def dot(a, b):
    return jnp.dot(a, b, preferred_element_type=F32)


def iota(shape, dim):
    return lax.broadcasted_iota(jnp.int32, shape, dim)


def one_hot(condition):
    return jnp.where(condition, 1.0, 0.0).astype(BF)


def kernel(
    a_hbm, b_hbm, w_hbm, bias_hbm, x_hbm, pair, gl_ref, gr_ref, gw_ref,
    a_own, b_own, w_own, bias, x, xt, wp, wpt, w32, mask, g, o, arep, arept, bp, bpt, b32, bs32,
    gwt, gr, gs32, rows32, fold, gather_s,
    a_all, b_all, w1_out, w1_in, w2_out, w2_in, l_out, l_in, r_out, r_in,
    own_sem, x_sem, send, recv,
):
    row, col = lax.axis_index("row"), lax.axis_index("col")

    y, z = row // 4, lax.rem(row, 4)
    u, zl, core = col // 4, lax.rem(col // 2, 2), lax.rem(col, 2)
    around, apart = (0, 1, 2, 1), (0, 2, 4, 2)
    row_steps = sorted(
        ((dy, dz) for dy in range(4) for dz in range(4) if dy or dz), key=lambda t: -around[t[0]] - apart[t[1]]
    )
    col_steps = sorted(
        ((dx, dz, dc) for dx in range(4) for dz in range(2) for dc in range(2) if dx or dz or dc),
        key=lambda t: -around[t[0]] - t[1],
    )
    row_peers = [lax.rem(y + dy, 4) * 4 + lax.rem(z + dz, 4) for dy, dz in row_steps]
    col_peers = [
        lax.rem(u + dx, 4) * 4 + lax.rem(zl + dz, 2) * 2 + lax.rem(core + dc, 2) for dx, dz, dc in col_steps
    ]

    def on_col(k):
        return (row, k)

    def on_row(k):
        return (k, col)

    def push(src, dst, which, device):
        pltpu.make_async_remote_copy(
            src_ref=src, dst_ref=dst, send_sem=send.at[which], recv_sem=recv.at[which],
            device_id=device, device_id_type=MESH,
        ).start()

    def others(peers, body):
        for k in peers:
            body(k)

    def wait_all(ref, sem):
        blocks = ref.at[pl.ds(0, N - 1)]
        pltpu.make_async_copy(blocks, blocks, sem).wait()

    A, B, W1, W2, GL, GR = range(6)

    loads = [
        pltpu.make_async_copy(src, dst, own_sem.at[n])
        for n, (src, dst) in enumerate(((a_hbm, a_own), (b_hbm, b_own), (w_hbm, w_own), (bias_hbm, bias)))
    ]
    for load in loads:
        load.start()

    barrier = pltpu.get_barrier_semaphore()

    def greet(k, to):
        pl.semaphore_signal(barrier, inc=1, device_id=to(k), device_id_type=MESH)

    others(row_peers, lambda k: greet(k, on_row))
    others(col_peers, lambda k: greet(k, on_col))

    def x_load(q):
        part = pl.ds(q * 16, 16)
        return pltpu.make_async_copy(x_hbm.at[part], x.at[part], x_sem.at[q])

    for q in range(4):
        x_load(q).start()

    mask[...] = one_hot(iota((256, 256), 0) // 32 == iota((256, 256), 1) // 32)
    m, n = iota((512, 128), 0), iota((512, 128), 1)
    fold[...] = one_hot((m // 128 == n // 32) & (m % 32 == n % 32))
    m, n = iota((16, 128), 0), iota((16, 128), 1)
    gather_s[...] = one_hot((m % 4 == n // 32) & (m // 4 == n % 32 // 8))
    same_block = iota((32, 128), 0) % 4 == iota((32, 128), 1) // 32
    same_dl = iota((128, 256), 0) % 8 == iota((128, 256), 1) // 32

    loads[0].wait()
    loads[1].wait()

    def unfolded(ref):
        parts = []
        for i in range(L):
            tiles = [
                jnp.broadcast_to(ref[pl.ds(i, 1), pl.ds(h * 128, 128)].astype(F32), (4, 128)) for h in range(8)
            ]
            parts.append(jnp.where(same_block, jnp.concatenate(tiles, axis=0), 0.0).astype(BF))
        return jnp.concatenate(parts, axis=1)

    own = dot(jnp.concatenate([unfolded(a_own), unfolded(b_own)], axis=0), fold[...])
    a_all[col] = own[0:32].astype(BF)
    spread_s = one_hot(iota((32, 256), 0) == iota((32, 256), 1) % 32)
    wide = jnp.where(same_dl, dot(own[32:64].T.astype(BF), spread_s), 0.0).astype(BF)
    b_all[row] = dot(gather_s[...], wide).astype(BF)

    pl.semaphore_wait(barrier, 2 * (N - 1))
    others(col_peers[:6], lambda k: push(a_all.at[col], a_all.at[col], A, on_col(k)))
    others(row_peers, lambda k: push(b_all.at[row], b_all.at[row], B, on_row(k)))
    others(col_peers[6:], lambda k: push(a_all.at[col], a_all.at[col], A, on_col(k)))

    loads[2].wait()
    loads[3].wait()
    w32[...] = w_own[...].astype(F32)
    for d in range(D):
        wp[pl.ds(d * C, C), :] = w32[pl.ds(d, C, stride=D), :].astype(BF)
    for q in range(8):
        wpt[:, pl.ds(q * 128, 128)] = wp[pl.ds(q * 128, 128), :].T

    def outer_grad(q):
        x_load(q).wait()
        rows = x[pl.ds(q * 16, 16)].reshape(16 * R, Z)
        part = dot(rows, wpt[...]).astype(BF)
        for dh in range(4):
            g[pl.ds(q * 16, 16), pl.ds(dh * R, R), :] = part[:, dh * 256 : dh * 256 + 256].reshape(16, R, 256)

    def x_transpose(q):
        for h in range(4):
            rows = x[pl.ds(q * 16 + h * 4, 4)].reshape(256, Z)
            xt[q, :, pl.ds(h * 256, 256)] = rows.T

    for q in range(4):
        outer_grad(q)
    for q in range(4):
        x_transpose(q)
    m, n = iota((128, 1024), 0), iota((128, 1024), 1)
    spread = jnp.where((m // 32 == n // 256) & (m % 32 == n % 32), SCALE, 0.0).astype(BF)

    wait_all(a_all, recv.at[A])
    arep[...] = dot(a_all[...].reshape(N * S, 128), spread).astype(BF).reshape(N, S, 1024)
    for q in range(4):
        turned = a_all[pl.ds(q * 4, 4)].reshape(128, 128).T
        arept[q] = dot(turned, spread).astype(BF)

    def diagonal(block):
        return jnp.concatenate([block] * 8, axis=0) * mask[...]

    wait_all(b_all, recv.at[B])
    bs32[...] = b_all[...].astype(F32)
    for q in range(N):
        for dh in range(4):
            b32[pl.ds(dh * R + q * L, L), :] = bs32[q, pl.ds(dh * L, L), :]
    bp[...] = b32[...].astype(BF)
    bpt[...] = b32[...].T.astype(BF)
    def outer(q, carry):
        for t in range(8):
            for i in range(L):
                rhs = diagonal(arep[q * 8 + t, :, pl.ds(i * 256, 256)])
                o[q * 32 + t * 4 + i] = dot(bp[...], rhs).astype(BF)
        return carry

    lax.fori_loop(0, 2, outer, 0)

    side = lax.rem(u, 2)
    for sx, sz in ((0, 1), (0, 0), (1, 1), (1, 0)):
        x1, z1 = lax.rem(side + sx, 2), lax.rem(zl + sz, 2)
        dh = x1 * 2 + z1
        rows = [o[pl.ds(q * 16, 16), pl.ds(dh * R, R), :].reshape(16 * R, 256) for q in range(4)]
        part = dot(xt[0], rows[0]) + dot(xt[1], rows[1]) + dot(xt[2], rows[2]) + dot(xt[3], rows[3])
        for h in range(2):
            gwt[pl.ds(h * 128, 128), :] = part[:, h * 128 : h * 128 + 128].T
        for up in (1, 0):
            for c1 in range(2):
                first_x = lax.rem(u + 2 * up, 4) if sx == 0 else x1 + 2 * up
                k = first_x * 4 + z1 * 2 + c1
                for dl in range(4):
                    first = (4 * c1 + dl) * C + first_x // 2
                    w1_out[k, pl.ds(dl * 16, 16), :] = gwt[pl.ds(first, 16, stride=2), :].astype(BF)

                @pl.when(k != col)
                def _():
                    push(w1_out.at[k], w1_in.at[col], W1, on_col(k))

    w1_in[col] = w1_out[col]

    gr[...] = jnp.zeros_like(gr)

    def right_grad(step, carry):
        for v in range(2):
            q = step * 2 + v
            lhs = jnp.concatenate([g[q * 16 + i] for i in range(16)], axis=1)
            rhs = jnp.concatenate(
                [diagonal(arept[q, pl.ds(i % 4 * 32, 32), pl.ds(i // 4 * 256, 256)]) for i in range(16)], axis=0
            )
            gr[...] += dot(lhs, rhs)
        return carry

    lax.fori_loop(0, 2, right_grad, 0)
    for q in range(N):
        for dh in range(4):
            gs32[q, pl.ds(dh * L, L), :] = gr[pl.ds(dh * R + q * L, L), :]
    r_out[...] = gs32[...].astype(BF)
    r_in[row] = r_out[row]
    others(row_peers, lambda k: push(r_out.at[k], r_in.at[row], GR, on_row(k)))

    lane4 = iota((32, 256), 1) % 128 // 32
    lane = iota((32, 128), 1) // 32

    def left_group(q):
        result = jnp.zeros((32, 128), F32)
        for two in range(2):
            i0 = q * L + two * 2
            both = jnp.zeros((32, 256), F32)
            for h in range(2):
                half = pl.ds(h * 128, 128)
                rhs = jnp.concatenate([g[i0, :, half], g[i0 + 1, :, half]], axis=1)
                part = dot(bpt[half, :], rhs)
                kept = part[96:128]
                for dl in range(3):
                    kept = jnp.where(lane4 == dl, part[dl * 32 : dl * 32 + 32], kept)
                both += kept
            for i in range(2):
                one = both[:, i * 128 : i * 128 + 128]
                one = one + pltpu.roll(one, 64, 1)
                one = one + pltpu.roll(one, 32, 1)
                result = jnp.where(lane == two * 2 + i, one, result)
        l_out[q] = result.astype(BF)

    def left_step(u, carry):
        for v in range(8):
            left_group(lax.rem(col + 8 * u + v + 1, N))
        for v in range(8):
            t = 8 * u + v + 1
            q = lax.rem(col + t, N)

            @pl.when(t < N)
            def _():
                push(l_out.at[q], l_in.at[col], GL, on_col(q))

        return carry

    lax.fori_loop(0, 2, left_step, 0)
    l_in[col] = l_out[col]

    wait_all(w1_in, recv.at[W1])
    total = w1_in[0].astype(F32)
    for k in range(1, N):
        total += w1_in[k].astype(F32)
    gwt[pl.ds(0, 64), :] = total
    for k in range(N):
        w2_out[k] = gwt[pl.ds(k, 4, stride=16), :]
    w2_in[row] = w2_out[row]
    others(row_peers, lambda k: push(w2_out.at[k], w2_in.at[row], W2, on_row(k)))

    for q in range(16):
        lhs = jnp.concatenate(
            [o[pl.ds(q * 4, 4), pl.ds(dh * R, R), :].reshape(4 * R, 256) for dh in range(4)], axis=1
        )
        total = dot(lhs, wp[...]) + bias[...]
        pair[pl.ds(q * 4, 4)] = total.astype(BF).reshape(4, R, Z)


    def folded(block):
        wide = lax.dot_general(block, fold[...], (((1,), (1,)), ((), ())), preferred_element_type=F32)
        kept = jnp.where(jnp.concatenate([same_block] * 4, axis=1), wide, 0.0).astype(BF)
        heads = one_hot(iota((8, 32), 0) == iota((8, 32), 1) // 4)
        tiles = dot(heads, kept)
        for i in range(L):
            for h in range(8):
                rows32[pl.ds(i, 1), pl.ds(h * 128, 128)] = tiles[h : h + 1, i * 128 : i * 128 + 128]
        return rows32[0:4, :].astype(BF)

    wait_all(r_in, recv.at[GR])
    total = r_in[0].astype(F32)
    for k in range(1, N):
        total += r_in[k].astype(F32)
    wide = lax.dot_general(
        gather_s[...], total.astype(BF), (((0,), (0,)), ((), ())), preferred_element_type=F32
    )
    wide = jnp.where(same_dl, wide, 0.0).astype(BF)
    by_s = lax.dot_general(spread_s, wide, (((1,), (1,)), ((), ())), preferred_element_type=F32)
    gr_ref[...] = folded(by_s.astype(BF))

    wait_all(l_in, recv.at[GL])
    total = l_in[0].astype(F32)
    for k in range(1, N):
        total += l_in[k].astype(F32)
    gl_ref[...] = folded((total * SCALE).astype(BF))

    for ref, which in ((a_all, A), (b_all, B), (w1_in, W1), (l_in, GL), (r_in, GR), (w2_in, W2)):
        wait_all(ref, send.at[which])

    wait_all(w2_in, recv.at[W2])
    total = w2_in[0]
    for k in range(1, N):
        total += w2_in[k]
    gw_ref[...] = total


def store(pair, gl, gr, gw, pair_hbm, gl_hbm, gr_hbm, gw_hbm, sem):
    copies = [pltpu.make_async_copy(src, dst, sem.at[n]) for n, (src, dst) in enumerate(
        [(pair.at[pl.ds(q * 8, 8)], pair_hbm.at[pl.ds(q * 8, 8)]) for q in range(8)]
        + [(gl, gl_hbm), (gr, gr_hbm), (gw, gw_hbm)])]
    for copy in copies:
        copy.start()
    for copy in copies:
        copy.wait()


def shards(a, b, w, bias, x):
    vmem = pl.BlockSpec(memory_space=pltpu.VMEM)
    hbm = pl.BlockSpec(memory_space=pltpu.HBM)
    v = pltpu.VMEM
    outs = (
        jax.ShapeDtypeStruct((R, R, Z), BF),
        jax.ShapeDtypeStruct((L, S * C), BF),
        jax.ShapeDtypeStruct((L, S * D), BF),
        jax.ShapeDtypeStruct((4, Z), F32),
    )
    results = pl.pallas_call(
        kernel,
        out_shape=outs,
        in_specs=[hbm] * 5,
        out_specs=(vmem,) * 4,
        scratch_shapes=[
            v((L, 1024), BF), v((L, 1024), BF), v((1024, Z), BF), v((1, Z), F32),
            v((R, R, Z), BF), v((4, Z, 1024), BF), v((1024, Z), BF), v((Z, 1024), BF), v((1024, Z), F32),
            v((256, 256), BF), v((R, 256, 256), BF), v((R, 256, 256), BF),
            v((N, S, 1024), BF), v((4, 128, 1024), BF),
            v((256, 256), BF), v((256, 256), BF), v((256, 256), F32), v((N, 16, 256), F32),
            v((256, Z), F32), v((256, 256), F32), v((N, 16, 256), F32),
            v((8, 1024), F32), v((512, 128), BF), v((16, 128), BF),
            v((N, S, 128), BF), v((N, 16, 256), BF),
            v((N, 64, Z), BF), v((N, 64, Z), BF), v((N, 4, Z), F32), v((N, 4, Z), F32),
            v((N, S, 128), BF), v((N, S, 128), BF), v((N, 16, 256), BF), v((N, 16, 256), BF),
            pltpu.SemaphoreType.DMA((4,)), pltpu.SemaphoreType.DMA((4,)),
            pltpu.SemaphoreType.DMA((6,)), pltpu.SemaphoreType.DMA((6,)),
        ],
        compiler_params=pltpu.CompilerParams(
            collective_id=0, has_side_effects=True, vmem_limit_bytes=48 * 2**20
        ),
        cost_estimate=pl.CostEstimate(
            flops=8_000_000_000, bytes_accessed=3_000_000, transcendentals=0
        ),
    )(*[pltpu.with_memory_space_constraint(t, pltpu.HBM) for t in (a, b, w, bias.reshape(1, Z), x)])
    return pl.pallas_call(
        store,
        out_shape=outs,
        in_specs=[vmem] * 4,
        out_specs=(hbm,) * 4,
        scratch_shapes=[pltpu.SemaphoreType.DMA((11,))],
        compiler_params=pltpu.CompilerParams(vmem_limit_bytes=2**20),
    )(*[pltpu.with_memory_space_constraint(t, pltpu.VMEM) for t in results])


def solution(mesh):
    in_specs = (P(("row", "col"), None), P(("col", "row"), None), P(), P(), P("row", "col", None))
    out_specs = (
        P("row", "col", None),
        P(("row", "col"), None),
        P(("col", "row"), None),
        P(("row", "col"), None),
    )
    return jax.shard_map(shards, mesh=mesh, in_specs=in_specs, out_specs=out_specs, check_vma=False)
```

```python
import jax
import jax.numpy as jnp
from jax import lax
from jax.experimental import pallas as pl
from jax.experimental.pallas import tpu as pltpu
from jax.sharding import PartitionSpec as P

MESH = pl.DeviceIdType.MESH
BF, F32 = jnp.bfloat16, jnp.float32
S, C, D, Z = 32, 32, 32, 128
N = 16
L = 4
R = N * L
SCALE = 1.0 / S


def dot(a, b):
    return jnp.dot(a, b, preferred_element_type=F32)


def iota(shape, dim):
    return lax.broadcasted_iota(jnp.int32, shape, dim)


def one_hot(condition):
    return jnp.where(condition, 1.0, 0.0).astype(BF)


def kernel(
    a_hbm, b_hbm, w_hbm, bias_hbm, x_hbm, pair, gl_ref, gr_ref, gw_ref,
    a_own, b_own, w_own, bias, x, xt, wp, wpt, w32, mask, g, o, arep, arept, bp, bpt, b32, bs32,
    gwt, gr, gs32, rows32, fold, gather_s,
    a_all, b_all, w1_out, w1_in, w2_out, w2_in, l_out, l_in, r_out, r_in,
    own_sem, x_sem, send, recv,
):
    row, col = lax.axis_index("row"), lax.axis_index("col")

    y, z = row // 4, lax.rem(row, 4)
    u, zl, core = col // 4, lax.rem(col // 2, 2), lax.rem(col, 2)
    around, apart = (0, 1, 2, 1), (0, 2, 4, 2)
    row_steps = sorted(
        ((dy, dz) for dy in range(4) for dz in range(4) if dy or dz), key=lambda t: -around[t[0]] - apart[t[1]]
    )
    col_steps = sorted(
        ((dx, dz, dc) for dx in range(4) for dz in range(2) for dc in range(2) if dx or dz or dc),
        key=lambda t: -around[t[0]] - t[1],
    )
    row_peers = [lax.rem(y + dy, 4) * 4 + lax.rem(z + dz, 4) for dy, dz in row_steps]
    col_peers = [
        lax.rem(u + dx, 4) * 4 + lax.rem(zl + dz, 2) * 2 + lax.rem(core + dc, 2) for dx, dz, dc in col_steps
    ]

    def on_col(k):
        return (row, k)

    def on_row(k):
        return (k, col)

    def push(src, dst, which, device):
        pltpu.make_async_remote_copy(
            src_ref=src, dst_ref=dst, send_sem=send.at[which], recv_sem=recv.at[which],
            device_id=device, device_id_type=MESH,
        ).start()

    def others(peers, body):
        for k in peers:
            body(k)

    def wait_all(ref, sem):
        blocks = ref.at[pl.ds(0, N - 1)]
        pltpu.make_async_copy(blocks, blocks, sem).wait()

    A, B, W1, W2, GL, GR = range(6)

    loads = [
        pltpu.make_async_copy(src, dst, own_sem.at[n])
        for n, (src, dst) in enumerate(((a_hbm, a_own), (b_hbm, b_own), (w_hbm, w_own), (bias_hbm, bias)))
    ]
    for load in loads:
        load.start()

    barrier = pltpu.get_barrier_semaphore()

    def greet(k, to):
        pl.semaphore_signal(barrier, inc=1, device_id=to(k), device_id_type=MESH)

    others(row_peers, lambda k: greet(k, on_row))
    others(col_peers, lambda k: greet(k, on_col))

    def x_load(q):
        part = pl.ds(q * 16, 16)
        return pltpu.make_async_copy(x_hbm.at[part], x.at[part], x_sem.at[q])

    for q in range(4):
        x_load(q).start()

    mask[...] = one_hot(iota((256, 256), 0) // 32 == iota((256, 256), 1) // 32)
    m, n = iota((512, 128), 0), iota((512, 128), 1)
    fold[...] = one_hot((m // 128 == n // 32) & (m % 32 == n % 32))
    m, n = iota((16, 128), 0), iota((16, 128), 1)
    gather_s[...] = one_hot((m % 4 == n // 32) & (m // 4 == n % 32 // 8))
    same_block = iota((32, 128), 0) % 4 == iota((32, 128), 1) // 32
    same_dl = iota((128, 256), 0) % 8 == iota((128, 256), 1) // 32

    loads[0].wait()
    loads[1].wait()

    def unfolded(ref):
        parts = []
        for i in range(L):
            tiles = [
                jnp.broadcast_to(ref[pl.ds(i, 1), pl.ds(h * 128, 128)].astype(F32), (4, 128)) for h in range(8)
            ]
            parts.append(jnp.where(same_block, jnp.concatenate(tiles, axis=0), 0.0).astype(BF))
        return jnp.concatenate(parts, axis=1)

    own = dot(jnp.concatenate([unfolded(a_own), unfolded(b_own)], axis=0), fold[...])
    a_all[col] = own[0:32].astype(BF)
    spread_s = one_hot(iota((32, 256), 0) == iota((32, 256), 1) % 32)
    wide = jnp.where(same_dl, dot(own[32:64].T.astype(BF), spread_s), 0.0).astype(BF)
    b_all[row] = dot(gather_s[...], wide).astype(BF)

    pl.semaphore_wait(barrier, 2 * (N - 1))
    others(col_peers, lambda k: push(a_all.at[col], a_all.at[col], A, on_col(k)))
    others(row_peers, lambda k: push(b_all.at[row], b_all.at[row], B, on_row(k)))

    loads[2].wait()
    loads[3].wait()
    w32[...] = w_own[...].astype(F32)
    for d in range(D):
        wp[pl.ds(d * C, C), :] = w32[pl.ds(d, C, stride=D), :].astype(BF)
    for q in range(8):
        wpt[:, pl.ds(q * 128, 128)] = wp[pl.ds(q * 128, 128), :].T

    def outer_grad(q):
        x_load(q).wait()
        rows = x[pl.ds(q * 16, 16)].reshape(16 * R, Z)
        part = dot(rows, wpt[...]).astype(BF)
        for dh in range(4):
            g[pl.ds(q * 16, 16), pl.ds(dh * R, R), :] = part[:, dh * 256 : dh * 256 + 256].reshape(16, R, 256)

    def x_transpose(q):
        for h in range(4):
            rows = x[pl.ds(q * 16 + h * 4, 4)].reshape(256, Z)
            xt[q, :, pl.ds(h * 256, 256)] = rows.T

    for q in range(4):
        outer_grad(q)
    for q in range(4):
        x_transpose(q)
    m, n = iota((128, 1024), 0), iota((128, 1024), 1)
    spread = jnp.where((m // 32 == n // 256) & (m % 32 == n % 32), SCALE, 0.0).astype(BF)

    wait_all(a_all, recv.at[A])
    arep[...] = dot(a_all[...].reshape(N * S, 128), spread).astype(BF).reshape(N, S, 1024)
    for q in range(4):
        turned = a_all[pl.ds(q * 4, 4)].reshape(128, 128).T
        arept[q] = dot(turned, spread).astype(BF)

    def diagonal(block):
        return jnp.concatenate([block] * 8, axis=0) * mask[...]

    wait_all(b_all, recv.at[B])
    bs32[...] = b_all[...].astype(F32)
    for q in range(N):
        for dh in range(4):
            b32[pl.ds(dh * R + q * L, L), :] = bs32[q, pl.ds(dh * L, L), :]
    bp[...] = b32[...].astype(BF)
    bpt[...] = b32[...].T.astype(BF)
    def outer(q, carry):
        for t in range(8):
            for i in range(L):
                rhs = diagonal(arep[q * 8 + t, :, pl.ds(i * 256, 256)])
                o[q * 32 + t * 4 + i] = dot(bp[...], rhs).astype(BF)
        return carry

    lax.fori_loop(0, 2, outer, 0)

    side = lax.rem(u, 2)
    for sx, sz in ((0, 1), (0, 0), (1, 1), (1, 0)):
        x1, z1 = lax.rem(side + sx, 2), lax.rem(zl + sz, 2)
        dh = x1 * 2 + z1
        rows = [o[pl.ds(q * 16, 16), pl.ds(dh * R, R), :].reshape(16 * R, 256) for q in range(4)]
        part = dot(xt[0], rows[0]) + dot(xt[1], rows[1]) + dot(xt[2], rows[2]) + dot(xt[3], rows[3])
        for h in range(2):
            gwt[pl.ds(h * 128, 128), :] = part[:, h * 128 : h * 128 + 128].T
        for up in (1, 0):
            for c1 in range(2):
                first_x = lax.rem(u + 2 * up, 4) if sx == 0 else x1 + 2 * up
                k = first_x * 4 + z1 * 2 + c1
                for dl in range(4):
                    first = (4 * c1 + dl) * C + first_x // 2
                    w1_out[k, pl.ds(dl * 16, 16), :] = gwt[pl.ds(first, 16, stride=2), :].astype(BF)

                @pl.when(k != col)
                def _():
                    push(w1_out.at[k], w1_in.at[col], W1, on_col(k))

    w1_in[col] = w1_out[col]

    gr[...] = jnp.zeros_like(gr)

    def right_grad(step, carry):
        for v in range(2):
            q = step * 2 + v
            lhs = jnp.concatenate([g[q * 16 + i] for i in range(16)], axis=1)
            rhs = jnp.concatenate(
                [diagonal(arept[q, pl.ds(i % 4 * 32, 32), pl.ds(i // 4 * 256, 256)]) for i in range(16)], axis=0
            )
            gr[...] += dot(lhs, rhs)
        return carry

    lax.fori_loop(0, 2, right_grad, 0)
    for q in range(N):
        for dh in range(4):
            gs32[q, pl.ds(dh * L, L), :] = gr[pl.ds(dh * R + q * L, L), :]
    r_out[...] = gs32[...].astype(BF)
    r_in[row] = r_out[row]
    others(row_peers, lambda k: push(r_out.at[k], r_in.at[row], GR, on_row(k)))

    lane4 = iota((32, 256), 1) % 128 // 32
    lane = iota((32, 128), 1) // 32

    def left_group(q):
        result = jnp.zeros((32, 128), F32)
        for two in range(2):
            i0 = q * L + two * 2
            both = jnp.zeros((32, 256), F32)
            for h in range(2):
                half = pl.ds(h * 128, 128)
                rhs = jnp.concatenate([g[i0, :, half], g[i0 + 1, :, half]], axis=1)
                part = dot(bpt[half, :], rhs)
                kept = part[96:128]
                for dl in range(3):
                    kept = jnp.where(lane4 == dl, part[dl * 32 : dl * 32 + 32], kept)
                both += kept
            for i in range(2):
                one = both[:, i * 128 : i * 128 + 128]
                one = one + pltpu.roll(one, 64, 1)
                one = one + pltpu.roll(one, 32, 1)
                result = jnp.where(lane == two * 2 + i, one, result)
        l_out[q] = result.astype(BF)

    def left_step(step, carry):
        for v in range(8):
            left_group(step * 8 + v)
        return carry

    lax.fori_loop(0, 2, left_step, 0)

    wait_all(w1_in, recv.at[W1])
    total = w1_in[0].astype(F32)
    for k in range(1, N):
        total += w1_in[k].astype(F32)
    gwt[pl.ds(0, 64), :] = total
    for k in range(N):
        w2_out[k] = gwt[pl.ds(k, 4, stride=16), :]
    w2_in[row] = w2_out[row]
    others(row_peers, lambda k: push(w2_out.at[k], w2_in.at[row], W2, on_row(k)))
    l_in[col] = l_out[col]
    others(col_peers, lambda k: push(l_out.at[k], l_in.at[col], GL, on_col(k)))

    for q in range(16):
        lhs = jnp.concatenate(
            [o[pl.ds(q * 4, 4), pl.ds(dh * R, R), :].reshape(4 * R, 256) for dh in range(4)], axis=1
        )
        total = dot(lhs, wp[...]) + bias[...]
        pair[pl.ds(q * 4, 4)] = total.astype(BF).reshape(4, R, Z)

    def folded(block):
        wide = lax.dot_general(block, fold[...], (((1,), (1,)), ((), ())), preferred_element_type=F32)
        kept = jnp.where(jnp.concatenate([same_block] * 4, axis=1), wide, 0.0).astype(BF)
        heads = one_hot(iota((8, 32), 0) == iota((8, 32), 1) // 4)
        tiles = dot(heads, kept)
        for i in range(L):
            for h in range(8):
                rows32[pl.ds(i, 1), pl.ds(h * 128, 128)] = tiles[h : h + 1, i * 128 : i * 128 + 128]
        return rows32[0:4, :].astype(BF)

    wait_all(r_in, recv.at[GR])
    total = r_in[0].astype(F32)
    for k in range(1, N):
        total += r_in[k].astype(F32)
    wide = lax.dot_general(
        gather_s[...], total.astype(BF), (((0,), (0,)), ((), ())), preferred_element_type=F32
    )
    wide = jnp.where(same_dl, wide, 0.0).astype(BF)
    by_s = lax.dot_general(spread_s, wide, (((1,), (1,)), ((), ())), preferred_element_type=F32)
    gr_ref[...] = folded(by_s.astype(BF))

    wait_all(l_in, recv.at[GL])
    total = l_in[0].astype(F32)
    for k in range(1, N):
        total += l_in[k].astype(F32)
    gl_ref[...] = folded((total * SCALE).astype(BF))

    for ref, which in ((a_all, A), (b_all, B), (w1_in, W1), (l_in, GL), (r_in, GR), (w2_in, W2)):
        wait_all(ref, send.at[which])

    wait_all(w2_in, recv.at[W2])
    total = w2_in[0]
    for k in range(1, N):
        total += w2_in[k]
    gw_ref[...] = total


def store(pair, gl, gr, gw, pair_hbm, gl_hbm, gr_hbm, gw_hbm, sem):
    copies = [pltpu.make_async_copy(src, dst, sem.at[n]) for n, (src, dst) in enumerate(
        [(pair.at[pl.ds(q * 32, 32)], pair_hbm.at[pl.ds(q * 32, 32)]) for q in range(2)]
        + [(gl, gl_hbm), (gr, gr_hbm), (gw, gw_hbm)])]
    for copy in copies:
        copy.start()
    for copy in copies:
        copy.wait()


def shards(a, b, w, bias, x):
    vmem = pl.BlockSpec(memory_space=pltpu.VMEM)
    hbm = pl.BlockSpec(memory_space=pltpu.HBM)
    v = pltpu.VMEM
    outs = (
        jax.ShapeDtypeStruct((R, R, Z), BF),
        jax.ShapeDtypeStruct((L, S * C), BF),
        jax.ShapeDtypeStruct((L, S * D), BF),
        jax.ShapeDtypeStruct((4, Z), F32),
    )
    results = pl.pallas_call(
        kernel,
        out_shape=outs,
        in_specs=[hbm] * 5,
        out_specs=(vmem,) * 4,
        scratch_shapes=[
            v((L, 1024), BF), v((L, 1024), BF), v((1024, Z), BF), v((1, Z), F32),
            v((R, R, Z), BF), v((4, Z, 1024), BF), v((1024, Z), BF), v((Z, 1024), BF), v((1024, Z), F32),
            v((256, 256), BF), v((R, 256, 256), BF), v((R, 256, 256), BF),
            v((N, S, 1024), BF), v((4, 128, 1024), BF),
            v((256, 256), BF), v((256, 256), BF), v((256, 256), F32), v((N, 16, 256), F32),
            v((256, Z), F32), v((256, 256), F32), v((N, 16, 256), F32),
            v((8, 1024), F32), v((512, 128), BF), v((16, 128), BF),
            v((N, S, 128), BF), v((N, 16, 256), BF),
            v((N, 64, Z), BF), v((N, 64, Z), BF), v((N, 4, Z), F32), v((N, 4, Z), F32),
            v((N, S, 128), BF), v((N, S, 128), BF), v((N, 16, 256), BF), v((N, 16, 256), BF),
            pltpu.SemaphoreType.DMA((4,)), pltpu.SemaphoreType.DMA((4,)),
            pltpu.SemaphoreType.DMA((6,)), pltpu.SemaphoreType.DMA((6,)),
        ],
        compiler_params=pltpu.CompilerParams(
            collective_id=0, has_side_effects=True, vmem_limit_bytes=48 * 2**20
        ),
        cost_estimate=pl.CostEstimate(
            flops=8_000_000_000, bytes_accessed=3_000_000, transcendentals=0
        ),
    )(*[pltpu.with_memory_space_constraint(t, pltpu.HBM) for t in (a, b, w, bias.reshape(1, Z), x)])
    return pl.pallas_call(
        store,
        out_shape=outs,
        in_specs=[vmem] * 4,
        out_specs=(hbm,) * 4,
        scratch_shapes=[pltpu.SemaphoreType.DMA((5,))],
        compiler_params=pltpu.CompilerParams(vmem_limit_bytes=2**20),
    )(*[pltpu.with_memory_space_constraint(t, pltpu.VMEM) for t in results])


def solution(mesh):
    in_specs = (P(("row", "col"), None), P(("col", "row"), None), P(), P(), P("row", "col", None))
    out_specs = (
        P("row", "col", None),
        P(("row", "col"), None),
        P(("col", "row"), None),
        P(("row", "col"), None),
    )
    return jax.shard_map(shards, mesh=mesh, in_specs=in_specs, out_specs=out_specs, check_vma=False)
```
